32 devices in a mesh: row: 8 (over z, y), col: 4 (over x, core).
Axes of the slice: x: 2, y: 2, z: 4, core: 2. Of those that a mesh axis runs over, the one named last changes fastest.
Arguments:
- object_field: float32 [2, 1024, 512], P(None, 'row', 'col'), may hold values from -5 to 5
- probe: float32 [2, 2, 256, 256], replicated, may hold values from -5 to 5
- amplitudes: float32 [8, 4, 2, 256, 256], P('row', 'col'), may hold values from 0.2 to 2.5
- offsets: int32 [8, 4, 2, 2], P('row', 'col'), may hold values from -128 to 0
Outputs:
- object_out: float32 [2, 1024, 512], P(None, 'row', 'col')
- probe_out: float32 [2, 2, 256, 256], replicated
The draws below stay inside these ranges and needn't reach their ends.
Inputs may be any that keep to these rules, and one draw needn't show every extreme that they name: `offsets`: each scan's 256 x 256 window starts at this offset from its own tile's anchor, so it reaches at most 128 pixels into neighbouring tiles.
All inputs are finite; a program needn't handle non-finite values.
Results may differ from the reference program's by a relative error of at most 0.0003.
Values sent between devices are 32-bit elements; how exact they have to be, the bound alone decides.
A program may use at most 128 MiB of HBM per device.

```python
import jax
import jax.numpy as jnp
from jax import lax

PROBE = 256
HALF = 128
MODES = 2
SCANS = 2
TILE = 128
ITERS = 2
GRID_ROWS = 8
GRID_COLS = 4
NY = 1024
NX = 512


def set_ends(values, stream_key, least, largest):
    longest = values.shape.index(max(values.shape))
    spots = []
    for shift in (0, 1):
        where = [jax.random.randint(jax.random.fold_in(stream_key, axis), (), 0, length) for axis, length in enumerate(values.shape)]
        where[longest] = (where[longest] + shift) % values.shape[longest]
        spots.append(tuple(where))
    return values.at[spots[0]].set(least).at[spots[1]].set(largest)


def levels(rng, extent, shards, least, top_value):
    def one(position, blocks):
        draws = jax.random.uniform(jax.random.fold_in(jax.random.fold_in(rng, 6), position), (blocks,), jnp.float32, least / len(shards), top_value / len(shards))
        return jnp.repeat(jnp.exp(draws), extent[position] // blocks).reshape((-1,) + (1,) * (len(extent) - position - 1))

    factor_of = one(*shards[0])
    for cut in shards[1:]:
        factor_of = factor_of * one(*cut)
    return factor_of


def centred(stream_key, shape, scale, most, shards=(), held_as=jnp.bfloat16):
    entries = scale * jax.random.normal(stream_key, shape, jnp.float32)
    if shards:
        entries = entries * levels(stream_key, shape, shards, -0.22, 0.18)
    return jnp.clip(entries, -most, most).astype(held_as)


def setup_inputs(seed: int = 0) -> dict:
    arg_keys = jax.random.split(jax.random.key(seed), 5)
    return {
        "object_field": centred(arg_keys[0], (2, NY, NX), 0.7, 5.0, ((1, 8), (2, 4)), jnp.float32),
        "probe": centred(arg_keys[1], (2, MODES, PROBE, PROBE), 0.7, 5.0, (), jnp.float32),
        "amplitudes": jnp.clip(0.2 + 2.3 * jax.random.uniform(arg_keys[2], (GRID_ROWS, GRID_COLS, SCANS, PROBE, PROBE), jnp.float32) ** levels(arg_keys[2], (GRID_ROWS, GRID_COLS, SCANS, PROBE, PROBE), ((0, 8), (1, 4)), -0.2, 0.2), 0.2, 2.5),
        "offsets": set_ends(jax.random.randint(arg_keys[3], (GRID_ROWS, GRID_COLS, SCANS, 2), -HALF, TILE - HALF + 1), jax.random.fold_in(arg_keys[3], 1), -HALF, TILE - HALF).astype(jnp.int32),
    }


FLOOR = 0.5
OBJECT_STEP = 0.5
OBJECT_REG = 0.5
PROBE_STEP = 1.0
PROBE_REG = 1.0

def reference(object_field, probe, amplitudes, offsets):
    rows_idx = lax.broadcasted_iota(jnp.int32, (GRID_ROWS, GRID_COLS, SCANS), 0)
    cols_idx = lax.broadcasted_iota(jnp.int32, (GRID_ROWS, GRID_COLS, SCANS), 1)
    row_starts = (rows_idx * TILE + offsets[..., 0] + HALF).reshape(-1).astype(jnp.int32)
    col_starts = (cols_idx * TILE + offsets[..., 1] + HALF).reshape(-1).astype(jnp.int32)
    measured = amplitudes.reshape(-1, PROBE, PROBE)
    zero_index = jnp.zeros((), jnp.int32)
    for iteration in range(ITERS):
        padded = jnp.pad(object_field, ((0, 0), (HALF, HALF), (HALF, HALF)))
        probe_wave = probe[0] + 1j * probe[1]
        probe_power = lax.optimization_barrier(jnp.sum(probe[0] * probe[0] + probe[1] * probe[1], axis=0))

        def visit_scan(state_in, record):
            grad_object, grad_probe, probe_weight = state_in
            row_start, col_start, amplitude = record
            corner = (zero_index, row_start.astype(jnp.int32), col_start.astype(jnp.int32))
            window = lax.dynamic_slice(padded, corner, (2, PROBE, PROBE))
            object_wave = window[0] + 1j * window[1]
            far_field = jnp.fft.fft2(probe_wave * object_wave[None], norm='ortho')
            intensity = lax.optimization_barrier(jnp.sum(far_field.real ** 2 + far_field.imag ** 2, axis=0))
            factor = amplitude / jnp.maximum(jnp.sqrt(intensity), FLOOR) - 1.0
            back_wave = jnp.fft.ifft2(far_field * factor[None], norm='ortho')
            obj_term = lax.optimization_barrier(jnp.sum(jnp.conj(probe_wave) * back_wave, axis=0))
            contrib = jnp.stack([obj_term.real, obj_term.imag, probe_power])
            current = lax.dynamic_slice(grad_object, corner, (3, PROBE, PROBE))
            grad_object = lax.dynamic_update_slice(grad_object, current + contrib, corner)
            probe_term = jnp.conj(object_wave)[None] * back_wave
            grad_probe = grad_probe + jnp.stack([probe_term.real, probe_term.imag])
            probe_weight = probe_weight + window[0] * window[0] + window[1] * window[1]
            return ((grad_object, grad_probe, probe_weight), None)
        start_state = (jnp.zeros((3, NY + 2 * HALF, NX + 2 * HALF), jnp.float32), jnp.zeros((2, MODES, PROBE, PROBE), jnp.float32), jnp.zeros((PROBE, PROBE), jnp.float32))
        (grad_object, grad_probe, probe_weight), _ = lax.scan(visit_scan, start_state, (row_starts, col_starts, measured))
        totals = grad_object[:, HALF:HALF + NY, HALF:HALF + NX]
        object_field = object_field + OBJECT_STEP * totals[0:2] / (totals[2:3] + OBJECT_REG)
        probe = probe + PROBE_STEP * grad_probe / (probe_weight + PROBE_REG)
    return (object_field, probe)
```

```python
import math

import jax
import jax.numpy as jnp
import numpy as np
import ml_dtypes
from jax import lax
from jax.experimental import pallas as pl
from jax.experimental.pallas import tpu as pltpu
from jax.sharding import PartitionSpec as P

ITERS = 2
FLOOR = 0.5
OBJECT_STEP = 0.5
OBJECT_REG = 0.5
PROBE_STEP = 1.0
PROBE_REG = 1.0
F32 = jnp.float32
BF16 = jnp.bfloat16


def padded_2(cells, sides, width):
    for axis, dim in sides:
        count = lax.axis_size(axis)
        ends = count - 1
        head = lax.slice_in_dim(cells, 0, width, axis=dim)
        tail = lax.slice_in_dim(cells, cells.shape[dim] - width, cells.shape[dim], axis=dim)
        cells = jnp.concatenate(
            [
                lax.ppermute(tail, axis, [(i, (i + 1) % count) for i in range(ends)]),
                cells,
                lax.ppermute(head, axis, [((i + 1) % count, i) for i in range(ends)]),
            ],
            axis=dim,
        )
    return cells


def split_np(table):
    high = table.astype(np.float32).astype(ml_dtypes.bfloat16)
    low = (table - high.astype(np.float64)).astype(np.float32).astype(ml_dtypes.bfloat16)
    return [high, low]


def tables(side):
    half = side // 2
    n = np.arange(half)[:, None]
    k = np.arange(half)[None, :]
    pieces = []
    for odd in (0, 1):
        angle = 2.0 * math.pi * ((n * (2 * k + odd)) % side) / side
        cos, sin = np.cos(angle) / math.sqrt(side), np.sin(angle) / math.sqrt(side)
        forward = np.block([[cos, -sin], [sin, cos]])
        pieces += split_np(forward) + split_np(forward.T)
    return np.stack(pieces)


def order_table(side):
    half = side // 2
    place = np.concatenate([2 * np.arange(half), 2 * np.arange(half) + 1])
    table = np.zeros((side, side), np.float32)
    table[place, np.arange(side)] = 1.0
    return np.stack([table, table.T]).astype(ml_dtypes.bfloat16)


def split(x):
    high = x.astype(BF16)
    return high, (x - high.astype(F32)).astype(BF16)


def dot(a, b):
    return jnp.dot(a, b, preferred_element_type=F32)


def right(x, tab, at):
    high, low = split(x)
    return dot(high, tab[at]) + (dot(high, tab[at + 1]) + dot(low, tab[at]))


def left(tab, at, x):
    high, low = split(x)
    return dot(tab[at], high) + (dot(tab[at + 1], high) + dot(tab[at], low))


FE, GE, FO, GO = 0, 2, 4, 6


def forward(re, im, tab):
    h = re.shape[1] // 2
    even = right(jnp.concatenate([re[:, :h] + re[:, h:], im[:, :h] + im[:, h:]], 1), tab, FE)
    odd = right(jnp.concatenate([re[:, :h] - re[:, h:], im[:, :h] - im[:, h:]], 1), tab, FO)
    re = jnp.concatenate([even[:, :h], odd[:, :h]], 1)
    im = jnp.concatenate([even[:, h:], odd[:, h:]], 1)
    even = left(tab, GE, jnp.concatenate([re[:h] + re[h:], im[:h] + im[h:]], 0))
    odd = left(tab, GO, jnp.concatenate([re[:h] - re[h:], im[:h] - im[h:]], 0))
    return (
        jnp.concatenate([even[:h], odd[:h]], 0),
        jnp.concatenate([even[h:], odd[h:]], 0),
    )


def inverse(re, im, tab):
    h = re.shape[1] // 2
    even = left(tab, FE, jnp.concatenate([re[:h], im[:h]], 0))
    odd = left(tab, FO, jnp.concatenate([re[h:], im[h:]], 0))
    low, high = even + odd, even - odd
    re = jnp.concatenate([low[:h], high[:h]], 0)
    im = jnp.concatenate([low[h:], high[h:]], 0)
    even = right(jnp.concatenate([re[:, :h], im[:, :h]], 1), tab, GE)
    odd = right(jnp.concatenate([re[:, h:], im[:, h:]], 1), tab, GO)
    low, high = even + odd, even - odd
    return (
        jnp.concatenate([low[:, :h], high[:, :h]], 1),
        jnp.concatenate([low[:, h:], high[:, h:]], 1),
    )


def step_kernel(starts, obj, probe, amp, tab, order, grad, pgrad, wide):
    side = probe.shape[2]
    full = obj.shape[1]
    modes = probe.shape[1]
    scans = amp.shape[0]
    wide[...] = jnp.zeros_like(wide)
    power = jnp.zeros((side, side), F32)
    for k in range(modes):
        power = power + probe[0, k] * probe[0, k] + probe[1, k] * probe[1, k]
    for s in range(scans):
        row, col = starts[s, 0], starts[s, 1]
        back_row, back_col = lax.rem(full - row, full), lax.rem(full - col, full)
        win = []
        for ch in range(2):
            x = pltpu.roll(obj[ch], back_row, 0)[:side]
            win.append(pltpu.roll(x, back_col, 1)[:, :side])
        wr, wi = win
        ordered = jnp.zeros((side, side), F32)
        for part in split(amp[s]):
            ordered = ordered + dot(order[1], dot(part, order[0]).astype(BF16))
        fars = []
        intensity = jnp.zeros((side, side), F32)
        for k in range(modes):
            pr, pi = probe[0, k], probe[1, k]
            fr, fi = forward(pr * wr - pi * wi, pr * wi + pi * wr, tab)
            intensity = intensity + fr * fr + fi * fi
            fars.append((fr, fi))
        factor = ordered / jnp.maximum(jnp.sqrt(intensity), FLOOR) - 1.0
        gr = jnp.zeros((side, side), F32)
        gi = jnp.zeros((side, side), F32)
        for k in range(modes):
            br, bi = inverse(fars[k][0] * factor, fars[k][1] * factor, tab)
            pr, pi = probe[0, k], probe[1, k]
            gr = gr + pr * br + pi * bi
            gi = gi + pr * bi - pi * br
            for ch, value in enumerate((wr * br + wi * bi, wr * bi - wi * br)):
                at = ch * modes + k
                pgrad[at] = value if s == 0 else pgrad[at] + value
        value = wr * wr + wi * wi
        pgrad[2 * modes] = value if s == 0 else pgrad[2 * modes] + value
        for ch, value in enumerate((gr, gi, power)):
            wide[:side, :side] = value
            x = pltpu.roll(pltpu.roll(wide[...], col, 1), row, 0)
            grad[ch] = x if s == 0 else grad[ch] + x


def step(starts, padded, probe, measured, tab, order):
    side = probe.shape[2]
    full = padded.shape[1]
    vmem = pl.BlockSpec(memory_space=pltpu.VMEM)
    flops = 2 * side**3 * 12 * 8
    return pl.pallas_call(
        step_kernel,
        out_shape=(
            jax.ShapeDtypeStruct((3, full, full), F32),
            jax.ShapeDtypeStruct((2 * probe.shape[1] + 1, side, side), F32),
        ),
        in_specs=[pl.BlockSpec(memory_space=pltpu.SMEM)] + [vmem] * 5,
        out_specs=(vmem, vmem),
        scratch_shapes=[pltpu.VMEM((full, full), F32)],
        compiler_params=pltpu.CompilerParams(vmem_limit_bytes=48 * 1024 * 1024),
        cost_estimate=pl.CostEstimate(flops=flops, bytes_accessed=6 << 20, transcendentals=0),
    )(starts, padded, probe, measured, tab, order)


def local(object_field, probe, amplitudes, offsets):
    tile = object_field.shape[1]
    modes = probe.shape[1]
    side = probe.shape[2]
    half = side // 2
    starts = offsets[0, 0] + half
    measured = amplitudes[0, 0]
    tab = jnp.asarray(tables(side))
    order = jnp.asarray(order_table(side))
    sides = (("row", 1), ("col", 2))
    for _ in range(ITERS):
        padded = padded_2(object_field, sides, half)
        grad, pgrad = step(starts, padded, probe, measured, tab, order)
        total = grad
        for axis, dim in sides:
            count = lax.axis_size(axis)
            low = lax.slice_in_dim(total, 0, half, axis=dim)
            own = lax.slice_in_dim(total, half, half + tile, axis=dim)
            high = lax.slice_in_dim(total, half + tile, 2 * half + tile, axis=dim)
            total = (
                own
                + lax.ppermute(high, axis, [(i, i + 1) for i in range(count - 1)])
                + lax.ppermute(low, axis, [(i + 1, i) for i in range(count - 1)])
            )
        pgrad = lax.psum(pgrad, ("row", "col"))
        summed = pgrad[: 2 * modes].reshape(probe.shape)
        probe = probe + PROBE_STEP * summed / (pgrad[2 * modes] + PROBE_REG)
        object_field = object_field + OBJECT_STEP * total[:2] / (total[2:] + OBJECT_REG)
    return object_field, probe


def solution(mesh):
    return jax.shard_map(
        local,
        mesh=mesh,
        in_specs=(
            P(None, "row", "col"),
            P(),
            P("row", "col", None, None, None),
            P("row", "col", None, None),
        ),
        out_specs=(P(None, "row", "col"), P()),
        check_vma=False,
    )
```

```python
import math

import jax
import jax.numpy as jnp
import numpy as np
import ml_dtypes
from jax import lax
from jax.experimental import pallas as pl
from jax.experimental.pallas import tpu as pltpu
from jax.sharding import PartitionSpec as P

ITERS = 2
FLOOR = 0.5
OBJECT_STEP = 0.5
OBJECT_REG = 0.5
PROBE_STEP = 1.0
PROBE_REG = 1.0
F32 = jnp.float32
BF16 = jnp.bfloat16


MESH = pl.DeviceIdType.MESH


def bits_of(axis, count):
    return [(axis, b) for b in range(count.bit_length() - 1)]


def stream_orders(rows, cols):
    row_bits, col_bits = bits_of("row", rows), bits_of("col", cols)
    one = col_bits + row_bits
    two = col_bits[:1] + row_bits[1:-1] + col_bits[1:] + row_bits[:1] + row_bits[-1:]
    return (one, two)


def plan(order, count):
    steps = []
    for axis, bit in order:
        halves = count % 2 == 0
        steps.append((axis, bit, count, halves))
        count = count // 2 if halves else count
    return steps


def bit_and_partner(axis, bit):
    me = lax.axis_index(axis)
    mine = lax.rem(me // (1 << bit), 2)
    return mine, {axis: me + (1 << bit) * (1 - 2 * mine)}


def remote(src, dst, sems, at, device):
    return pltpu.make_async_remote_copy(
        src_ref=src, dst_ref=dst, send_sem=sems.at[0, at], recv_sem=sems.at[1, at],
        device_id=device, device_id_type=MESH,
    )


def greet(rows, cols, bits):
    barrier = pltpu.get_barrier_semaphore()
    row, col = lax.axis_index("row"), lax.axis_index("col")
    devices = [
        {"row": lax.rem(row + 1, rows)}, {"row": lax.rem(row + rows - 1, rows)},
        {"col": lax.rem(col + 1, cols)}, {"col": lax.rem(col + cols - 1, cols)},
    ] + [bit_and_partner(axis, bit)[1] for axis, bit in bits]
    for device in devices:
        pl.semaphore_signal(barrier, inc=1, device_id=device, device_id_type=MESH)
    pl.semaphore_wait(barrier, len(devices))


class Pair:
    def __init__(self, axis, count, sems, at, up, down):
        me = lax.axis_index(axis)
        self.not_last, self.not_first = me < count - 1, me > 0
        self.up = remote(up[0], up[1], sems, at, {axis: jnp.minimum(me + 1, count - 1)})
        self.down = remote(down[0], down[1], sems, at + 1, {axis: jnp.maximum(me - 1, 0)})

    def start(self):
        pl.when(self.not_last)(self.up.start)
        pl.when(self.not_first)(self.down.start)

    def wait(self):
        pl.when(self.not_first)(self.up.wait_recv)
        pl.when(self.not_last)(self.down.wait_recv)

    def wait_sent(self):
        pl.when(self.not_last)(self.up.wait_send)
        pl.when(self.not_first)(self.down.wait_send)


def row_halo(tile_ref, pad, sems, at, rows, tile, half):
    own = pl.ds(half, tile)
    return Pair(
        "row", rows, sems, at,
        (tile_ref, pad.at[:, pl.ds(0, half), own]),
        (tile_ref, pad.at[:, pl.ds(half + tile, half), own]),
    )


def col_halo(pad, sems, at, cols, tile, half):
    own = pl.ds(half, tile)
    return Pair(
        "col", cols, sems, at,
        (pad.at[:, :, own], pad.at[:, :, pl.ds(0, half)]),
        (pad.at[:, :, own], pad.at[:, :, pl.ds(half + tile, half)]),
    )


def clear_rim(pad, rows, cols, tile, half):
    row, col = lax.axis_index("row"), lax.axis_index("col")
    own = pl.ds(half, tile)

    def clear(*where):
        def run():
            pad[where] = jnp.zeros_like(pad[where])
        return run

    every = slice(None)
    pl.when(row == 0)(clear(every, pl.ds(0, half), own))
    pl.when(row == rows - 1)(clear(every, pl.ds(half + tile, half), own))
    pl.when(col == 0)(clear(every, every, pl.ds(0, half)))
    pl.when(col == cols - 1)(clear(every, every, pl.ds(half + tile, half)))


def halo_kernel(rows, cols, obj, out, pad, sems):
    tile = obj.shape[1]
    half = (pad.shape[1] - tile) // 2
    greet(rows, cols, ())
    by_row = row_halo(obj, pad, sems, 0, rows, tile, half)
    by_row.start()
    clear_rim(pad, rows, cols, tile, half)
    pad[:, pl.ds(half, tile), pl.ds(half, tile)] = obj[...]
    by_row.wait()
    by_col = col_halo(pad, sems, 2, cols, tile, half)
    by_col.start()
    by_col.wait()
    by_row.wait_sent()
    by_col.wait_sent()
    out[...] = pad[...]


def halo(rows, cols, obj, half):
    full = obj.shape[1] + 2 * half
    vmem = pl.BlockSpec(memory_space=pltpu.VMEM)
    return pl.pallas_call(
        lambda *refs: halo_kernel(rows, cols, *refs),
        out_shape=jax.ShapeDtypeStruct((2, full, full), F32),
        in_specs=[vmem],
        out_specs=vmem,
        scratch_shapes=[pltpu.VMEM((2, full, full), F32), pltpu.SemaphoreType.DMA((2, 4))],
        compiler_params=pltpu.CompilerParams(
            collective_id=0, has_side_effects=True, vmem_limit_bytes=32 * 1024 * 1024
        ),
    )(obj)


def exchange_kernel(rows, cols, last, obj, probe, grad, pgrad, *refs):
    if last:
        obj_out, probe_out, colbuf, mid, rowbuf, new_obj, acc, inbox, res, gsems, rsems, asems = refs
    else:
        (obj_out, probe_out, pad_out, colbuf, mid, rowbuf, new_obj, acc, inbox, res,
         gsems, rsems, asems, pad, hsems) = refs
    tile = obj.shape[1]
    full = grad.shape[1]
    half = (full - tile) // 2
    row, col = lax.axis_index("row"), lax.axis_index("col")
    orders = stream_orders(rows, cols)
    greet(rows, cols, orders[0])
    spots = pgrad.shape[0] // len(orders)
    plans = [plan(order, spots) for order in orders]
    los = [s * spots for s in range(len(orders))]
    box = 0
    reduces, gathers = [], []
    for s, steps in enumerate(plans):
        for step, (axis, bit, count, halves) in enumerate(steps):
            n = count // 2 if halves else count
            mine, device = bit_and_partner(axis, bit)
            lo = los[s]
            keep = lo + mine * n if halves else lo
            send = lo + (1 - mine) * n if halves else lo
            source = pgrad if step == 0 else acc
            buf = inbox.at[pl.ds(box, n)]
            box += n
            copy = remote(source.at[pl.ds(send, n)], buf, rsems.at[s], step, device)
            reduces.append((step, copy, source, keep, n, buf))
            if halves:
                span = res.at[pl.ds(keep, n)]
                gathers.append((s, step, remote(span, span, asems.at[s], step, device)))
                los[s] = keep

    def start_reduce(at):
        for step, copy, *_ in reduces:
            if step == at:
                copy.start()

    def finish_reduce(at):
        for step, copy, source, keep, n, buf in reduces:
            if step == at:
                copy.wait()
                acc[pl.ds(keep, n)] = source[pl.ds(keep, n)] + buf[...]

    total_steps = len(plans[0])
    start_reduce(0)
    by_col = Pair(
        "col", cols, gsems, 0,
        (grad.at[:, :, pl.ds(half + tile, half)], colbuf.at[0]),
        (grad.at[:, :, pl.ds(0, half)], colbuf.at[1]),
    )
    by_row = Pair(
        "row", rows, gsems, 2,
        (mid.at[:, pl.ds(half + tile, half)], rowbuf.at[0]),
        (mid.at[:, pl.ds(0, half)], rowbuf.at[1]),
    )
    by_col.start()

    def clear(ref, at):
        def run():
            ref[at] = jnp.zeros_like(ref[at])
        return run

    pl.when(col == 0)(clear(colbuf, 0))
    pl.when(col == cols - 1)(clear(colbuf, 1))
    pl.when(row == 0)(clear(rowbuf, 0))
    pl.when(row == rows - 1)(clear(rowbuf, 1))
    if not last:
        clear_rim(pad, rows, cols, tile, half)

    finish_reduce(0)
    start_reduce(1)
    by_col.wait()
    mid[...] = grad[:, :, half:half + tile] + colbuf[0] + colbuf[1]
    by_row.start()
    finish_reduce(1)
    start_reduce(2)
    by_row.wait()
    total = mid[:, half:half + tile] + rowbuf[0] + rowbuf[1]
    new = obj[...] + OBJECT_STEP * total[:2] / (total[2:] + OBJECT_REG)
    new_obj[...] = new
    obj_out[...] = new
    if not last:
        halo_row = row_halo(new_obj, pad, hsems, 0, rows, tile, half)
        halo_col = col_halo(pad, hsems, 2, cols, tile, half)
        halo_row.start()
        pad[:, pl.ds(half, tile), pl.ds(half, tile)] = new
    finish_reduce(2)
    start_reduce(3)
    if not last:
        halo_row.wait()
        halo_col.start()
    for step in range(3, total_steps):
        finish_reduce(step)
        if step + 1 < total_steps:
            start_reduce(step + 1)
    for s, steps in enumerate(plans):
        _, _, count, halves = steps[-1]
        n = count // 2 if halves else count
        span = pl.ds(los[s], n)
        terms = acc[span]
        channels = probe.shape[1]
        res[span] = probe[span] + PROBE_STEP * terms[:, :channels] / (
            terms[:, channels:] + PROBE_REG
        )
    for at in reversed(range(total_steps)):
        now = [copy for s, step, copy in gathers if step == at]
        for copy in now:
            copy.start()
        for copy in now:
            copy.wait()
    by_col.wait_sent()
    by_row.wait_sent()
    probe_out[...] = res[...]
    if not last:
        halo_col.wait()
        halo_row.wait_sent()
        halo_col.wait_sent()
        pad_out[...] = pad[...]


def exchange(rows, cols, last, obj, probe, grad, pgrad):
    tile, full = obj.shape[1], grad.shape[1]
    half = (full - tile) // 2
    channels = grad.shape[0]
    orders = stream_orders(rows, cols)
    spots = pgrad.shape[0] // len(orders)
    boxes = sum(
        count // 2 if halves else count
        for order in orders
        for _, _, count, halves in plan(order, spots)
    )
    steps = len(orders[0])
    vmem = pl.BlockSpec(memory_space=pltpu.VMEM)
    out_shape = [jax.ShapeDtypeStruct(obj.shape, F32), jax.ShapeDtypeStruct(probe.shape, F32)]
    scratch = [
        pltpu.VMEM((2, channels, full, half), F32),
        pltpu.VMEM((channels, full, tile), F32),
        pltpu.VMEM((2, channels, half, tile), F32),
        pltpu.VMEM(obj.shape, F32),
        pltpu.VMEM(pgrad.shape, F32),
        pltpu.VMEM((boxes,) + pgrad.shape[1:], F32),
        pltpu.VMEM(probe.shape, F32),
        pltpu.SemaphoreType.DMA((2, 4)),
        pltpu.SemaphoreType.DMA((len(orders), 2, steps)),
        pltpu.SemaphoreType.DMA((len(orders), 2, steps)),
    ]
    if not last:
        out_shape.append(jax.ShapeDtypeStruct((2, full, full), F32))
        scratch += [pltpu.VMEM((2, full, full), F32), pltpu.SemaphoreType.DMA((2, 4))]
    return pl.pallas_call(
        lambda *refs: exchange_kernel(rows, cols, last, *refs),
        out_shape=out_shape,
        in_specs=[vmem] * 4,
        out_specs=[vmem] * len(out_shape),
        scratch_shapes=scratch,
        compiler_params=pltpu.CompilerParams(
            collective_id=2 if last else 1,
            has_side_effects=True,
            vmem_limit_bytes=48 * 1024 * 1024,
        ),
    )(obj, probe, grad, pgrad)


def split_np(table):
    high = table.astype(np.float32).astype(ml_dtypes.bfloat16)
    low = (table - high.astype(np.float64)).astype(np.float32).astype(ml_dtypes.bfloat16)
    return [high, low]


def tables(side):
    half = side // 2
    n = np.arange(half)[:, None]
    k = np.arange(half)[None, :]
    pieces = []
    for odd in (0, 1):
        angle = 2.0 * math.pi * ((n * (2 * k + odd)) % side) / side
        cos, sin = np.cos(angle) / math.sqrt(side), np.sin(angle) / math.sqrt(side)
        forward = np.block([[cos, -sin], [sin, cos]])
        pieces += split_np(forward) + split_np(forward.T)
    return np.stack(pieces)


def order_table(side):
    half = side // 2
    place = np.concatenate([2 * np.arange(half), 2 * np.arange(half) + 1])
    table = np.zeros((side, side), np.float32)
    table[place, np.arange(side)] = 1.0
    return np.stack([table, table.T]).astype(ml_dtypes.bfloat16)


def split(x):
    high = x.astype(BF16)
    return high, (x - high.astype(F32)).astype(BF16)


def dot(a, b):
    return jnp.dot(a, b, preferred_element_type=F32)


def right(x, tab, at):
    high, low = split(x)
    return dot(high, tab[at]) + (dot(high, tab[at + 1]) + dot(low, tab[at]))


def left(tab, at, x):
    high, low = split(x)
    return dot(tab[at], high) + (dot(tab[at + 1], high) + dot(tab[at], low))


FE, GE, FO, GO = 0, 2, 4, 6


def forward(re, im, tab):
    h = re.shape[1] // 2
    even = right(jnp.concatenate([re[:, :h] + re[:, h:], im[:, :h] + im[:, h:]], 1), tab, FE)
    odd = right(jnp.concatenate([re[:, :h] - re[:, h:], im[:, :h] - im[:, h:]], 1), tab, FO)
    re = jnp.concatenate([even[:, :h], odd[:, :h]], 1)
    im = jnp.concatenate([even[:, h:], odd[:, h:]], 1)
    even = left(tab, GE, jnp.concatenate([re[:h] + re[h:], im[:h] + im[h:]], 0))
    odd = left(tab, GO, jnp.concatenate([re[:h] - re[h:], im[:h] - im[h:]], 0))
    return (
        jnp.concatenate([even[:h], odd[:h]], 0),
        jnp.concatenate([even[h:], odd[h:]], 0),
    )


def inverse(re, im, tab):
    h = re.shape[1] // 2
    even = left(tab, FE, jnp.concatenate([re[:h], im[:h]], 0))
    odd = left(tab, FO, jnp.concatenate([re[h:], im[h:]], 0))
    low, high = even + odd, even - odd
    re = jnp.concatenate([low[:h], high[:h]], 0)
    im = jnp.concatenate([low[h:], high[h:]], 0)
    even = right(jnp.concatenate([re[:, :h], im[:, :h]], 1), tab, GE)
    odd = right(jnp.concatenate([re[:, h:], im[:, h:]], 1), tab, GO)
    low, high = even + odd, even - odd
    return (
        jnp.concatenate([low[:, :h], high[:, :h]], 1),
        jnp.concatenate([low[:, h:], high[:, h:]], 1),
    )


def whole(tiles, at, side):
    blocks = tiles.shape[0] * tiles.shape[2] // side
    per = tiles.shape[0] // blocks
    return jnp.concatenate(
        [tiles[j * per:(j + 1) * per, at].reshape(side, -1) for j in range(blocks)], 1
    )


def put(tiles, at, value, add):
    width = tiles.shape[3]
    per = value.shape[0] // tiles.shape[2]
    for j in range(value.shape[1] // width):
        part = value[:, j * width:(j + 1) * width].reshape(per, tiles.shape[2], width)
        span = slice(j * per, (j + 1) * per)
        tiles[span, at] = tiles[span, at] + part if add else part


def step_kernel(starts, obj, tiles, amp, tab, order, grad, pgrad, wide):
    side = amp.shape[1]
    full = obj.shape[1]
    modes = tiles.shape[1] // 2
    scans = amp.shape[0]
    probe = {(c, k): whole(tiles, c * modes + k, side) for c in range(2) for k in range(modes)}
    wide[...] = jnp.zeros_like(wide)
    power = jnp.zeros((side, side), F32)
    for k in range(modes):
        power = power + probe[0, k] * probe[0, k] + probe[1, k] * probe[1, k]
    for s in range(scans):
        row, col = starts[s, 0], starts[s, 1]
        back_row, back_col = lax.rem(full - row, full), lax.rem(full - col, full)
        win = []
        for ch in range(2):
            x = pltpu.roll(obj[ch], back_row, 0)[:side]
            win.append(pltpu.roll(x, back_col, 1)[:, :side])
        wr, wi = win
        ordered = jnp.zeros((side, side), F32)
        for part in split(amp[s]):
            ordered = ordered + dot(order[1], dot(part, order[0]).astype(BF16))
        fars = []
        intensity = jnp.zeros((side, side), F32)
        for k in range(modes):
            pr, pi = probe[0, k], probe[1, k]
            fr, fi = forward(pr * wr - pi * wi, pr * wi + pi * wr, tab)
            intensity = intensity + fr * fr + fi * fi
            fars.append((fr, fi))
        factor = ordered / jnp.maximum(jnp.sqrt(intensity), FLOOR) - 1.0
        gr = jnp.zeros((side, side), F32)
        gi = jnp.zeros((side, side), F32)
        for k in range(modes):
            br, bi = inverse(fars[k][0] * factor, fars[k][1] * factor, tab)
            pr, pi = probe[0, k], probe[1, k]
            gr = gr + pr * br + pi * bi
            gi = gi + pr * bi - pi * br
            for ch, value in enumerate((wr * br + wi * bi, wr * bi - wi * br)):
                at = ch * modes + k
                put(pgrad, at, value, s > 0)
        put(pgrad, 2 * modes, wr * wr + wi * wi, s > 0)
        for ch, value in enumerate((gr, gi, power)):
            wide[:side, :side] = value
            x = pltpu.roll(pltpu.roll(wide[...], col, 1), row, 0)
            grad[ch] = x if s == 0 else grad[ch] + x


def step(starts, padded, probe, measured, tab, order):
    side = measured.shape[1]
    full = padded.shape[1]
    vmem = pl.BlockSpec(memory_space=pltpu.VMEM)
    flops = 2 * side**3 * 12 * 8
    return pl.pallas_call(
        step_kernel,
        out_shape=(
            jax.ShapeDtypeStruct((3, full, full), F32),
            jax.ShapeDtypeStruct((probe.shape[0], probe.shape[1] + 1) + probe.shape[2:], F32),
        ),
        in_specs=[pl.BlockSpec(memory_space=pltpu.SMEM)] + [vmem] * 5,
        out_specs=(vmem, vmem),
        scratch_shapes=[pltpu.VMEM((full, full), F32)],
        compiler_params=pltpu.CompilerParams(vmem_limit_bytes=48 * 1024 * 1024),
        cost_estimate=pl.CostEstimate(flops=flops, bytes_accessed=6 << 20, transcendentals=0),
    )(starts, padded, probe, measured, tab, order)


def local(object_field, probe, amplitudes, offsets):
    side = probe.shape[2]
    half = side // 2
    rows, cols = lax.axis_size("row"), lax.axis_size("col")
    starts = offsets[0, 0] + half
    measured = amplitudes[0, 0]
    tab = jnp.asarray(tables(side))
    order = jnp.asarray(order_table(side))
    channels = probe.shape[0] * probe.shape[1]
    cut = (channels, side // 8, 8, side // 128, 128)
    tiles = probe.reshape(cut).transpose(3, 1, 0, 2, 4).reshape(-1, channels, 8, 128)
    padded = halo(rows, cols, object_field, half)
    for iteration in range(ITERS):
        last = iteration + 1 == ITERS
        grad, pgrad = step(starts, padded, tiles, measured, tab, order)
        out = exchange(rows, cols, last, object_field, tiles, grad, pgrad)
        object_field, tiles = out[:2]
        if not last:
            padded = out[2]
    back = tiles.reshape(side // 128, side // 8, channels, 8, 128).transpose(2, 1, 3, 0, 4)
    return object_field, back.reshape(probe.shape)


def solution(mesh):
    return jax.shard_map(
        local,
        mesh=mesh,
        in_specs=(
            P(None, "row", "col"),
            P(),
            P("row", "col", None, None, None),
            P("row", "col", None, None),
        ),
        out_specs=(P(None, "row", "col"), P()),
        check_vma=False,
    )
```

```python
import math

import jax
import jax.numpy as jnp
import numpy as np
import ml_dtypes
from jax import lax
from jax.experimental import pallas as pl
from jax.experimental.pallas import tpu as pltpu
from jax.sharding import PartitionSpec as P

ITERS = 2
FLOOR = 0.5
OBJECT_STEP = 0.5
OBJECT_REG = 0.5
PROBE_STEP = 1.0
PROBE_REG = 1.0
F32 = jnp.float32
BF16 = jnp.bfloat16
STREAMS = 2
ABSENT = 1 << 20


MESH = pl.DeviceIdType.MESH


def bits_of(axis, count):
    return [(axis, b) for b in range(count.bit_length() - 1)]


def phases(rows, cols):
    row_bits, col_bits = bits_of("row", rows), bits_of("col", cols)
    rest = row_bits[1:] + col_bits[2:]
    groups = [col_bits[:1], col_bits[1:2] + row_bits[:1]]
    return groups + [rest[i:i + 2] for i in range(0, len(rest), 2)]


def plan(groups, count):
    steps = []
    for group in groups:
        if count % (1 << len(group)) == 0:
            count //= 1 << len(group)
            steps.append((group, True, count))
        else:
            steps += [([bit], False, count) for bit in group]
    return steps


def peer(group, mask):
    device, mine, theirs = {}, 0, 0
    for i, (axis, bit) in enumerate(group):
        me = lax.axis_index(axis)
        held = lax.rem(me // (1 << bit), 2)
        mine = mine + held * (1 << i)
        if mask >> i & 1:
            device[axis] = device.get(axis, me) + (1 << bit) * (1 - 2 * held)
            theirs = theirs + (1 - held) * (1 << i)
        else:
            theirs = theirs + held * (1 << i)
    return device, mine, theirs


def remote(src, dst, sems, at, device):
    return pltpu.make_async_remote_copy(
        src_ref=src, dst_ref=dst, send_sem=sems.at[(0,) + at], recv_sem=sems.at[(1,) + at],
        device_id=device, device_id_type=MESH,
    )


def greet(rows, cols, groups):
    barrier = pltpu.get_barrier_semaphore()
    row, col = lax.axis_index("row"), lax.axis_index("col")
    devices = [
        {"row": lax.rem(row + 1, rows)}, {"row": lax.rem(row + rows - 1, rows)},
        {"col": lax.rem(col + 1, cols)}, {"col": lax.rem(col + cols - 1, cols)},
    ]
    for group in groups:
        devices += [peer(group, mask)[0] for mask in range(1, 1 << len(group))]
    for device in devices:
        pl.semaphore_signal(barrier, inc=1, device_id=device, device_id_type=MESH)
    pl.semaphore_wait(barrier, len(devices))


class Pair:
    def __init__(self, axis, count, sems, at, up, down):
        me = lax.axis_index(axis)
        self.not_last, self.not_first = me < count - 1, me > 0
        self.up = remote(up[0], up[1], sems, (at,), {axis: jnp.minimum(me + 1, count - 1)})
        self.down = remote(down[0], down[1], sems, (at + 1,), {axis: jnp.maximum(me - 1, 0)})

    def start(self):
        pl.when(self.not_last)(self.up.start)
        pl.when(self.not_first)(self.down.start)

    def wait(self):
        pl.when(self.not_first)(self.up.wait_recv)
        pl.when(self.not_last)(self.down.wait_recv)

    def wait_sent(self):
        pl.when(self.not_last)(self.up.wait_send)
        pl.when(self.not_first)(self.down.wait_send)


def row_halo(tile_ref, pad, sems, at, rows, tile, half):
    own = pl.ds(half, tile)
    return Pair(
        "row", rows, sems, at,
        (tile_ref, pad.at[:, pl.ds(0, half), own]),
        (tile_ref, pad.at[:, pl.ds(half + tile, half), own]),
    )


def col_halo(pad, sems, at, cols, tile, half):
    own = pl.ds(half, tile)
    return Pair(
        "col", cols, sems, at,
        (pad.at[:, :, own], pad.at[:, :, pl.ds(0, half)]),
        (pad.at[:, :, own], pad.at[:, :, pl.ds(half + tile, half)]),
    )


def clear_rim(pad, rows, cols, tile, half):
    row, col = lax.axis_index("row"), lax.axis_index("col")
    own = pl.ds(half, tile)

    def clear(*where):
        def run():
            pad[where] = jnp.zeros_like(pad[where])
        return run

    every = slice(None)
    pl.when(row == 0)(clear(every, pl.ds(0, half), own))
    pl.when(row == rows - 1)(clear(every, pl.ds(half + tile, half), own))
    pl.when(col == 0)(clear(every, every, pl.ds(0, half)))
    pl.when(col == cols - 1)(clear(every, every, pl.ds(half + tile, half)))


def halo_kernel(rows, cols, obj, offs, out, near_out, pad, near, sems):
    tile = obj.shape[1]
    half = (pad.shape[1] - tile) // 2
    greet(rows, cols, ())
    by_row = row_halo(obj, pad, sems, 0, rows, tile, half)
    by_row.start()
    offs_row = Pair("row", rows, sems, 4, (offs, near.at[1, 0]), (offs, near.at[1, 2]))
    offs_row.start()
    near[1, 1] = offs[...]
    row, col = lax.axis_index("row"), lax.axis_index("col")

    def absent(*where):
        def run():
            near[where] = jnp.full_like(near[where], ABSENT)
        return run

    pl.when(row == 0)(absent(1, 0))
    pl.when(row == rows - 1)(absent(1, 2))
    pl.when(col == 0)(absent(0))
    pl.when(col == cols - 1)(absent(2))
    clear_rim(pad, rows, cols, tile, half)
    pad[:, pl.ds(half, tile), pl.ds(half, tile)] = obj[...]
    by_row.wait()
    by_col = col_halo(pad, sems, 2, cols, tile, half)
    by_col.start()
    offs_row.wait()
    offs_col = Pair("col", cols, sems, 6, (near.at[1], near.at[0]), (near.at[1], near.at[2]))
    offs_col.start()
    by_col.wait()
    offs_col.wait()
    for pair in (by_row, by_col, offs_row, offs_col):
        pair.wait_sent()
    out[...] = pad[...]
    near_out[...] = near[...]


def halo(rows, cols, obj, offs, half):
    full = obj.shape[1] + 2 * half
    vmem = pl.BlockSpec(memory_space=pltpu.VMEM)
    return pl.pallas_call(
        lambda *refs: halo_kernel(rows, cols, *refs),
        out_shape=(
            jax.ShapeDtypeStruct((2, full, full), F32),
            jax.ShapeDtypeStruct((3, 3) + offs.shape, jnp.int32),
        ),
        in_specs=[vmem, vmem],
        out_specs=(vmem, vmem),
        scratch_shapes=[
            pltpu.VMEM((2, full, full), F32),
            pltpu.VMEM((3, 3) + offs.shape, jnp.int32),
            pltpu.SemaphoreType.DMA((2, 8)),
        ],
        compiler_params=pltpu.CompilerParams(
            collective_id=0, has_side_effects=True, vmem_limit_bytes=32 * 1024 * 1024
        ),
    )(obj, offs)


def weight_of(probe, near, scans, tile):
    channels = probe.shape[1]
    power = probe[:, 0] * probe[:, 0]
    for at in range(1, channels):
        power = power + probe[:, at] * probe[:, at]
    side = math.isqrt(power.size)
    power = whole(power[:, None], 0, side)
    both = jnp.concatenate(split(power), 1)
    along = lax.broadcasted_iota(jnp.int32, (tile, side), 0) - lax.broadcasted_iota(
        jnp.int32, (tile, side), 1
    )
    across = lax.broadcasted_iota(jnp.int32, (side, tile), 1) - lax.broadcasted_iota(
        jnp.int32, (side, tile), 0
    )
    weight = jnp.zeros((tile, tile), F32)
    for dc in range(3):
        for dr in range(3):
            for s in range(scans):
                top = near[dc, dr, 2 * s:2 * s + 1, :] + (dr - 1) * tile
                edge = near[dc, dr, 2 * s + 1:2 * s + 2, :] + (dc - 1) * tile
                top = jnp.concatenate([top] * (side // top.shape[1]), 1)
                pick = jnp.where(along == top, 1.0, 0.0).astype(BF16)
                place = jnp.where(across == edge, 1.0, 0.0).astype(BF16)
                cut = dot(pick, both)
                high, low = split(cut[:, :side] + cut[:, side:])
                weight = weight + (dot(high, place) + dot(low, place))
    return weight


def exchange_kernel(rows, cols, last, scans, obj, probe, near, grad, pgrad, *refs):
    if last:
        obj_out, probe_out, colbuf, mid, rowbuf, new_obj, acc, inbox, res, gsems, rsems, asems = refs
    else:
        (obj_out, probe_out, pad_out, colbuf, mid, rowbuf, new_obj, acc, inbox, res,
         gsems, rsems, asems, pad, hsems) = refs
    tile = obj.shape[1]
    full = grad.shape[1]
    half = (full - tile) // 2
    row, col = lax.axis_index("row"), lax.axis_index("col")
    groups = phases(rows, cols)
    greet(rows, cols, groups)
    spots = pgrad.shape[0] // STREAMS
    steps = plan(groups, spots)
    box = 0
    reduces, gathers, ends = {}, {}, []
    for s in range(STREAMS):
        lo = s * spots
        for step, (group, scatters, n) in enumerate(steps):
            source = pgrad if step == 0 else acc
            _, mine, _ = peer(group, 0)
            keep = lo + mine * n if scatters else lo
            copies, spread = [], []
            for mask in range(1, 1 << len(group)):
                device, _, theirs = peer(group, mask)
                send = lo + theirs * n if scatters else lo
                buf = inbox.at[pl.ds(box, n)]
                box += n
                at = (step, mask - 1)
                copies.append((remote(source.at[pl.ds(send, n)], buf, rsems.at[s], at, device), buf))
                if scatters:
                    span = res.at[pl.ds(keep, n)]
                    spread.append(remote(span, span, asems.at[s], at, device))
            reduces[s, step] = (copies, source, keep, n)
            gathers[s, step] = spread
            lo = keep
        ends.append(lo)
    total_steps = len(steps)

    def start_reduce(s, step):
        for copy, _ in reduces[s, step][0]:
            copy.start()

    def advance(step):
        for s in range(STREAMS):
            copies, source, keep, n = reduces[s, step]
            for copy, _ in copies:
                copy.wait()
            value = source[pl.ds(keep, n)]
            for _, buf in copies:
                value = value + buf[...]
            if step + 1 < total_steps:
                acc[pl.ds(keep, n)] = value
                start_reduce(s, step + 1)
            else:
                channels = probe.shape[1]
                res[pl.ds(keep, n)] = probe[pl.ds(keep, n)] + PROBE_STEP * value[:, :channels] / (
                    value[:, channels:] + PROBE_REG
                )
                start_gather(s, step)

    def start_gather(s, step):
        for copy in gathers[s, step]:
            copy.start()

    def back(step):
        for s in range(STREAMS):
            for copy in gathers[s, step]:
                copy.wait()
            if step:
                start_gather(s, step - 1)

    for s in range(STREAMS):
        start_reduce(s, 0)
    by_col = Pair(
        "col", cols, gsems, 0,
        (grad.at[:, :, pl.ds(half + tile, half)], colbuf.at[0]),
        (grad.at[:, :, pl.ds(0, half)], colbuf.at[1]),
    )
    by_row = Pair(
        "row", rows, gsems, 2,
        (mid.at[:, pl.ds(half + tile, half)], rowbuf.at[0]),
        (mid.at[:, pl.ds(0, half)], rowbuf.at[1]),
    )
    by_col.start()

    def clear(ref, at):
        def run():
            ref[at] = jnp.zeros_like(ref[at])
        return run

    pl.when(col == 0)(clear(colbuf, 0))
    pl.when(col == cols - 1)(clear(colbuf, 1))
    pl.when(row == 0)(clear(rowbuf, 0))
    pl.when(row == rows - 1)(clear(rowbuf, 1))
    if not last:
        clear_rim(pad, rows, cols, tile, half)

    advance(0)
    weight = weight_of(probe, near, scans, tile)
    by_col.wait()
    mid[...] = grad[:, :, half:half + tile] + colbuf[0] + colbuf[1]
    by_row.start()
    advance(1)
    by_row.wait()
    total = mid[:, half:half + tile] + rowbuf[0] + rowbuf[1]
    new = obj[...] + OBJECT_STEP * total / (weight + OBJECT_REG)
    new_obj[...] = new
    obj_out[...] = new
    if not last:
        halo_row = row_halo(new_obj, pad, hsems, 0, rows, tile, half)
        halo_col = col_halo(pad, hsems, 2, cols, tile, half)
        halo_row.start()
        pad[:, pl.ds(half, tile), pl.ds(half, tile)] = new
    for step in range(2, total_steps):
        advance(step)
    if not last:
        halo_row.wait()
        halo_col.start()
    for step in reversed(range(total_steps)):
        back(step)
    by_col.wait_sent()
    by_row.wait_sent()
    probe_out[...] = res[...]
    if not last:
        halo_col.wait()
        halo_row.wait_sent()
        halo_col.wait_sent()
        pad_out[...] = pad[...]


def exchange(rows, cols, last, scans, obj, probe, near, grad, pgrad):
    tile, full = obj.shape[1], grad.shape[1]
    half = (full - tile) // 2
    channels = grad.shape[0]
    steps = plan(phases(rows, cols), pgrad.shape[0] // STREAMS)
    boxes = STREAMS * sum(n * ((1 << len(group)) - 1) for group, _, n in steps)
    most = max((1 << len(group)) - 1 for group, _, _ in steps)
    vmem = pl.BlockSpec(memory_space=pltpu.VMEM)
    out_shape = [jax.ShapeDtypeStruct(obj.shape, F32), jax.ShapeDtypeStruct(probe.shape, F32)]
    scratch = [
        pltpu.VMEM((2, channels, full, half), F32),
        pltpu.VMEM((channels, full, tile), F32),
        pltpu.VMEM((2, channels, half, tile), F32),
        pltpu.VMEM(obj.shape, F32),
        pltpu.VMEM(pgrad.shape, F32),
        pltpu.VMEM((boxes,) + pgrad.shape[1:], F32),
        pltpu.VMEM(probe.shape, F32),
        pltpu.SemaphoreType.DMA((2, 4)),
        pltpu.SemaphoreType.DMA((STREAMS, 2, len(steps), most)),
        pltpu.SemaphoreType.DMA((STREAMS, 2, len(steps), most)),
    ]
    if not last:
        out_shape.append(jax.ShapeDtypeStruct((2, full, full), F32))
        scratch += [pltpu.VMEM((2, full, full), F32), pltpu.SemaphoreType.DMA((2, 4))]
    return pl.pallas_call(
        lambda *refs: exchange_kernel(rows, cols, last, scans, *refs),
        out_shape=out_shape,
        in_specs=[vmem] * 5,
        out_specs=[vmem] * len(out_shape),
        scratch_shapes=scratch,
        compiler_params=pltpu.CompilerParams(
            collective_id=2 if last else 1,
            has_side_effects=True,
            vmem_limit_bytes=48 * 1024 * 1024,
        ),
    )(obj, probe, near, grad, pgrad)


def split_np(table):
    high = table.astype(np.float32).astype(ml_dtypes.bfloat16)
    low = (table - high.astype(np.float64)).astype(np.float32).astype(ml_dtypes.bfloat16)
    return [high, low]


def tables(side):
    half = side // 2
    n = np.arange(half)[:, None]
    k = np.arange(half)[None, :]
    pieces = []
    for odd in (0, 1):
        angle = 2.0 * math.pi * ((n * (2 * k + odd)) % side) / side
        cos, sin = np.cos(angle) / math.sqrt(side), np.sin(angle) / math.sqrt(side)
        forward = np.block([[cos, -sin], [sin, cos]])
        pieces += split_np(forward) + split_np(forward.T)
    return np.stack(pieces)


def order_table(side):
    half = side // 2
    place = np.concatenate([2 * np.arange(half), 2 * np.arange(half) + 1])
    table = np.zeros((side, side), np.float32)
    table[place, np.arange(side)] = 1.0
    return np.stack([table, table.T]).astype(ml_dtypes.bfloat16)


def split(x):
    high = x.astype(BF16)
    return high, (x - high.astype(F32)).astype(BF16)


def dot(a, b):
    return jnp.dot(a, b, preferred_element_type=F32)


def right(x, tab, at):
    high, low = split(x)
    return dot(high, tab[at]) + (dot(high, tab[at + 1]) + dot(low, tab[at]))


def left(tab, at, x):
    high, low = split(x)
    return dot(tab[at], high) + (dot(tab[at + 1], high) + dot(tab[at], low))


FE, GE, FO, GO = 0, 2, 4, 6


def forward(re, im, tab):
    h = re.shape[1] // 2
    even = right(jnp.concatenate([re[:, :h] + re[:, h:], im[:, :h] + im[:, h:]], 1), tab, FE)
    odd = right(jnp.concatenate([re[:, :h] - re[:, h:], im[:, :h] - im[:, h:]], 1), tab, FO)
    re = jnp.concatenate([even[:, :h], odd[:, :h]], 1)
    im = jnp.concatenate([even[:, h:], odd[:, h:]], 1)
    even = left(tab, GE, jnp.concatenate([re[:h] + re[h:], im[:h] + im[h:]], 0))
    odd = left(tab, GO, jnp.concatenate([re[:h] - re[h:], im[:h] - im[h:]], 0))
    return (
        jnp.concatenate([even[:h], odd[:h]], 0),
        jnp.concatenate([even[h:], odd[h:]], 0),
    )


def inverse(re, im, tab):
    h = re.shape[1] // 2
    even = left(tab, FE, jnp.concatenate([re[:h], im[:h]], 0))
    odd = left(tab, FO, jnp.concatenate([re[h:], im[h:]], 0))
    low, high = even + odd, even - odd
    re = jnp.concatenate([low[:h], high[:h]], 0)
    im = jnp.concatenate([low[h:], high[h:]], 0)
    even = right(jnp.concatenate([re[:, :h], im[:, :h]], 1), tab, GE)
    odd = right(jnp.concatenate([re[:, h:], im[:, h:]], 1), tab, GO)
    low, high = even + odd, even - odd
    return (
        jnp.concatenate([low[:, :h], high[:, :h]], 1),
        jnp.concatenate([low[:, h:], high[:, h:]], 1),
    )


def whole(tiles, at, side):
    blocks = tiles.shape[0] * tiles.shape[2] // side
    per = tiles.shape[0] // blocks
    return jnp.concatenate(
        [tiles[j * per:(j + 1) * per, at].reshape(side, -1) for j in range(blocks)], 1
    )


def put(tiles, at, value, add):
    width = tiles.shape[3]
    per = value.shape[0] // tiles.shape[2]
    for j in range(value.shape[1] // width):
        part = value[:, j * width:(j + 1) * width].reshape(per, tiles.shape[2], width)
        span = slice(j * per, (j + 1) * per)
        tiles[span, at] = tiles[span, at] + part if add else part


def step_kernel(starts, obj, tiles, amp, tab, order, grad, pgrad, wide):
    side = amp.shape[1]
    full = obj.shape[1]
    modes = tiles.shape[1] // 2
    scans = amp.shape[0]
    probe = {(c, k): whole(tiles, c * modes + k, side) for c in range(2) for k in range(modes)}
    wide[...] = jnp.zeros_like(wide)
    for s in range(scans):
        row, col = starts[s, 0] + side // 2, starts[s, 1] + side // 2
        back_row, back_col = lax.rem(full - row, full), lax.rem(full - col, full)
        win = []
        for ch in range(2):
            x = pltpu.roll(obj[ch], back_row, 0)[:side]
            win.append(pltpu.roll(x, back_col, 1)[:, :side])
        wr, wi = win
        ordered = jnp.zeros((side, side), F32)
        for part in split(amp[s]):
            ordered = ordered + dot(order[1], dot(part, order[0]).astype(BF16))
        fars = []
        intensity = jnp.zeros((side, side), F32)
        for k in range(modes):
            pr, pi = probe[0, k], probe[1, k]
            fr, fi = forward(pr * wr - pi * wi, pr * wi + pi * wr, tab)
            intensity = intensity + fr * fr + fi * fi
            fars.append((fr, fi))
        factor = ordered / jnp.maximum(jnp.sqrt(intensity), FLOOR) - 1.0
        gr = jnp.zeros((side, side), F32)
        gi = jnp.zeros((side, side), F32)
        for k in range(modes):
            br, bi = inverse(fars[k][0] * factor, fars[k][1] * factor, tab)
            pr, pi = probe[0, k], probe[1, k]
            gr = gr + pr * br + pi * bi
            gi = gi + pr * bi - pi * br
            for ch, value in enumerate((wr * br + wi * bi, wr * bi - wi * br)):
                at = ch * modes + k
                put(pgrad, at, value, s > 0)
        put(pgrad, 2 * modes, wr * wr + wi * wi, s > 0)
        for ch, value in enumerate((gr, gi)):
            wide[:side, :side] = value
            x = pltpu.roll(pltpu.roll(wide[...], col, 1), row, 0)
            grad[ch] = x if s == 0 else grad[ch] + x


def step(starts, padded, probe, measured, tab, order):
    side = measured.shape[1]
    full = padded.shape[1]
    vmem = pl.BlockSpec(memory_space=pltpu.VMEM)
    flops = 2 * side**3 * 12 * 8
    return pl.pallas_call(
        step_kernel,
        out_shape=(
            jax.ShapeDtypeStruct((2, full, full), F32),
            jax.ShapeDtypeStruct((probe.shape[0], probe.shape[1] + 1) + probe.shape[2:], F32),
        ),
        in_specs=[pl.BlockSpec(memory_space=pltpu.SMEM)] + [vmem] * 5,
        out_specs=(vmem, vmem),
        scratch_shapes=[pltpu.VMEM((full, full), F32)],
        compiler_params=pltpu.CompilerParams(vmem_limit_bytes=48 * 1024 * 1024),
        cost_estimate=pl.CostEstimate(flops=flops, bytes_accessed=6 << 20, transcendentals=0),
    )(starts, padded, probe, measured, tab, order)


def local(object_field, probe, amplitudes, offsets):
    side = probe.shape[2]
    half = side // 2
    rows, cols = lax.axis_size("row"), lax.axis_size("col")
    starts = offsets[0, 0]
    scans = starts.shape[0]
    measured = amplitudes[0, 0]
    tab = jnp.asarray(tables(side))
    order = jnp.asarray(order_table(side))
    channels = probe.shape[0] * probe.shape[1]
    cut = (channels, side // 8, 8, side // 128, 128)
    tiles = probe.reshape(cut).transpose(3, 1, 0, 2, 4).reshape(-1, channels, 8, 128)
    offs = jnp.broadcast_to(starts.reshape(-1, 1), (2 * scans, 128))
    padded, near = halo(rows, cols, object_field, offs, half)
    for iteration in range(ITERS):
        last = iteration + 1 == ITERS
        grad, pgrad = step(starts, padded, tiles, measured, tab, order)
        out = exchange(rows, cols, last, scans, object_field, tiles, near, grad, pgrad)
        object_field, tiles = out[:2]
        if not last:
            padded = out[2]
    back = tiles.reshape(side // 128, side // 8, channels, 8, 128).transpose(2, 1, 3, 0, 4)
    return object_field, back.reshape(probe.shape)


def solution(mesh):
    return jax.shard_map(
        local,
        mesh=mesh,
        in_specs=(
            P(None, "row", "col"),
            P(),
            P("row", "col", None, None, None),
            P("row", "col", None, None),
        ),
        out_specs=(P(None, "row", "col"), P()),
        check_vma=False,
    )
```

```python
import math

import jax
import jax.numpy as jnp
import numpy as np
import ml_dtypes
from jax import lax
from jax.experimental import pallas as pl
from jax.experimental.pallas import tpu as pltpu
from jax.sharding import PartitionSpec as P

ITERS = 2
FLOOR = 0.5
OBJECT_STEP = 0.5
OBJECT_REG = 0.5
PROBE_STEP = 1.0
PROBE_REG = 1.0
F32 = jnp.float32
BF16 = jnp.bfloat16
STREAMS = 2
ABSENT = 1 << 20


MESH = pl.DeviceIdType.MESH


def bits_of(axis, count):
    return [(axis, b) for b in range(count.bit_length() - 1)]


def phases(rows, cols):
    row_bits, col_bits = bits_of("row", rows), bits_of("col", cols)
    rest = row_bits[1:] + col_bits[2:]
    first, near = col_bits[:1], col_bits[1:2] + row_bits[:1]
    one = [first, near] + [rest[i:i + 2] for i in range(0, len(rest), 2)]
    late = rest[1:]
    two = [first, rest[:1], near] + [late[i:i + 2] for i in range(0, len(late), 2)]
    return [one, two]


def plan(groups, count):
    steps = []
    for group in groups:
        if count % (1 << len(group)) == 0:
            count //= 1 << len(group)
            steps.append((group, True, count))
        else:
            steps += [([bit], False, count) for bit in group]
    return steps


def peer(group, mask):
    device, mine, theirs = {}, 0, 0
    for i, (axis, bit) in enumerate(group):
        me = lax.axis_index(axis)
        held = lax.rem(me // (1 << bit), 2)
        mine = mine + held * (1 << i)
        if mask >> i & 1:
            device[axis] = device.get(axis, me) + (1 << bit) * (1 - 2 * held)
            theirs = theirs + (1 - held) * (1 << i)
        else:
            theirs = theirs + held * (1 << i)
    return device, mine, theirs


def remote(src, dst, sems, at, device):
    return pltpu.make_async_remote_copy(
        src_ref=src, dst_ref=dst, send_sem=sems.at[(0,) + at], recv_sem=sems.at[(1,) + at],
        device_id=device, device_id_type=MESH,
    )


def greet(rows, cols, groups):
    barrier = pltpu.get_barrier_semaphore()
    row, col = lax.axis_index("row"), lax.axis_index("col")
    devices = [
        {"row": lax.rem(row + 1, rows)}, {"row": lax.rem(row + rows - 1, rows)},
        {"col": lax.rem(col + 1, cols)}, {"col": lax.rem(col + cols - 1, cols)},
    ]
    known = []
    for group in groups:
        for mask in range(1, 1 << len(group)):
            flipped = sorted(item for i, item in enumerate(group) if mask >> i & 1)
            if flipped not in known:
                known.append(flipped)
                devices.append(peer(group, mask)[0])
    for device in devices:
        pl.semaphore_signal(barrier, inc=1, device_id=device, device_id_type=MESH)
    pl.semaphore_wait(barrier, len(devices))


class Pair:
    def __init__(self, axis, count, sems, at, up, down):
        me = lax.axis_index(axis)
        self.not_last, self.not_first = me < count - 1, me > 0
        self.up = remote(up[0], up[1], sems, (at,), {axis: jnp.minimum(me + 1, count - 1)})
        self.down = remote(down[0], down[1], sems, (at + 1,), {axis: jnp.maximum(me - 1, 0)})

    def start(self):
        pl.when(self.not_last)(self.up.start)
        pl.when(self.not_first)(self.down.start)

    def wait(self):
        pl.when(self.not_first)(self.up.wait_recv)
        pl.when(self.not_last)(self.down.wait_recv)

    def wait_sent(self):
        pl.when(self.not_last)(self.up.wait_send)
        pl.when(self.not_first)(self.down.wait_send)


def row_halo(tile_ref, pad, sems, at, rows, tile, half):
    own = pl.ds(half, tile)
    return Pair(
        "row", rows, sems, at,
        (tile_ref, pad.at[:, pl.ds(0, half), own]),
        (tile_ref, pad.at[:, pl.ds(half + tile, half), own]),
    )


def col_halo(pad, sems, at, cols, tile, half):
    own = pl.ds(half, tile)
    return Pair(
        "col", cols, sems, at,
        (pad.at[:, :, own], pad.at[:, :, pl.ds(0, half)]),
        (pad.at[:, :, own], pad.at[:, :, pl.ds(half + tile, half)]),
    )


def clear_rim(pad, rows, cols, tile, half):
    row, col = lax.axis_index("row"), lax.axis_index("col")
    own = pl.ds(half, tile)

    def clear(*where):
        def run():
            pad[where] = jnp.zeros_like(pad[where])
        return run

    every = slice(None)
    pl.when(row == 0)(clear(every, pl.ds(0, half), own))
    pl.when(row == rows - 1)(clear(every, pl.ds(half + tile, half), own))
    pl.when(col == 0)(clear(every, every, pl.ds(0, half)))
    pl.when(col == cols - 1)(clear(every, every, pl.ds(half + tile, half)))


def halo_kernel(rows, cols, obj, offs, probe, out, near_out, tiles, pad, near, sems):
    tile = obj.shape[1]
    half = (pad.shape[1] - tile) // 2
    greet(rows, cols, ())
    by_row = row_halo(obj, pad, sems, 0, rows, tile, half)
    by_row.start()
    offs_row = Pair("row", rows, sems, 4, (offs, near.at[1, 0]), (offs, near.at[1, 2]))
    offs_row.start()
    near[1, 1] = offs[...]
    row, col = lax.axis_index("row"), lax.axis_index("col")

    def absent(*where):
        def run():
            near[where] = jnp.full_like(near[where], ABSENT)
        return run

    pl.when(row == 0)(absent(1, 0))
    pl.when(row == rows - 1)(absent(1, 2))
    pl.when(col == 0)(absent(0))
    pl.when(col == cols - 1)(absent(2))
    clear_rim(pad, rows, cols, tile, half)
    pad[:, pl.ds(half, tile), pl.ds(half, tile)] = obj[...]
    for at in range(probe.shape[0]):
        put(tiles, at, probe[at], False)
    by_row.wait()
    by_col = col_halo(pad, sems, 2, cols, tile, half)
    by_col.start()
    offs_row.wait()
    offs_col = Pair("col", cols, sems, 6, (near.at[1], near.at[0]), (near.at[1], near.at[2]))
    offs_col.start()
    by_col.wait()
    offs_col.wait()
    for pair in (by_row, by_col, offs_row, offs_col):
        pair.wait_sent()
    out[...] = pad[...]
    near_out[...] = near[...]


def halo(rows, cols, obj, offs, probe, half):
    full = obj.shape[1] + 2 * half
    vmem = pl.BlockSpec(memory_space=pltpu.VMEM)
    return pl.pallas_call(
        lambda *refs: halo_kernel(rows, cols, *refs),
        out_shape=(
            jax.ShapeDtypeStruct((2, full, full), F32),
            jax.ShapeDtypeStruct((3, 3) + offs.shape, jnp.int32),
            jax.ShapeDtypeStruct((probe[0].size // 1024, probe.shape[0], 8, 128), F32),
        ),
        in_specs=[vmem, vmem, vmem],
        out_specs=(vmem, vmem, vmem),
        scratch_shapes=[
            pltpu.VMEM((2, full, full), F32),
            pltpu.VMEM((3, 3) + offs.shape, jnp.int32),
            pltpu.SemaphoreType.DMA((2, 8)),
        ],
        compiler_params=pltpu.CompilerParams(
            collective_id=0, has_side_effects=True, vmem_limit_bytes=32 * 1024 * 1024
        ),
    )(obj, offs, probe)


def weight_of(probe, near, scans, tile):
    channels = probe.shape[1]
    power = probe[:, 0] * probe[:, 0]
    for at in range(1, channels):
        power = power + probe[:, at] * probe[:, at]
    side = math.isqrt(power.size)
    power = whole(power[:, None], 0, side)
    both = jnp.concatenate(split(power), 1)
    along = lax.broadcasted_iota(jnp.int32, (tile, side), 0) - lax.broadcasted_iota(
        jnp.int32, (tile, side), 1
    )
    across = lax.broadcasted_iota(jnp.int32, (side, tile), 1) - lax.broadcasted_iota(
        jnp.int32, (side, tile), 0
    )
    weight = jnp.zeros((tile, tile), F32)
    for dc in range(3):
        for dr in range(3):
            for s in range(scans):
                top = near[dc, dr, 2 * s:2 * s + 1, :] + (dr - 1) * tile
                edge = near[dc, dr, 2 * s + 1:2 * s + 2, :] + (dc - 1) * tile
                top = jnp.concatenate([top] * (side // top.shape[1]), 1)
                pick = jnp.where(along == top, 1.0, 0.0).astype(BF16)
                place = jnp.where(across == edge, 1.0, 0.0).astype(BF16)
                cut = dot(pick, both)
                high, low = split(cut[:, :side] + cut[:, side:])
                weight = weight + (dot(high, place) + dot(low, place))
    return weight


def exchange_kernel(rows, cols, last, scans, obj, probe, near, grad, pgrad, *refs):
    if last:
        obj_out, probe_out, colbuf, mid, rowbuf, new_obj, acc, inbox, res, gsems, rsems, asems = refs
    else:
        (obj_out, probe_out, pad_out, colbuf, mid, rowbuf, new_obj, acc, inbox, res,
         gsems, rsems, asems, pad, hsems) = refs
    tile = obj.shape[1]
    full = grad.shape[1]
    half = (full - tile) // 2
    row, col = lax.axis_index("row"), lax.axis_index("col")
    groups = phases(rows, cols)
    greet(rows, cols, [group for stream in groups for group in stream])
    spots = pgrad.shape[0] // STREAMS
    plans = [plan(group, spots) for group in groups]
    box = 0
    reduces, gathers, ends = {}, {}, []
    for s in range(STREAMS):
        lo = s * spots
        for step, (group, scatters, n) in enumerate(plans[s]):
            source = pgrad if step == 0 else acc
            _, mine, _ = peer(group, 0)
            keep = lo + mine * n if scatters else lo
            copies, spread = [], []
            for mask in range(1, 1 << len(group)):
                device, _, theirs = peer(group, mask)
                send = lo + theirs * n if scatters else lo
                buf = inbox.at[pl.ds(box, n)]
                box += n
                at = (step, mask - 1)
                copies.append((remote(source.at[pl.ds(send, n)], buf, rsems.at[s], at, device), buf))
                if scatters:
                    span = res.at[pl.ds(keep, n)]
                    spread.append(remote(span, span, asems.at[s], at, device))
            reduces[s, step] = (copies, source, keep, n)
            gathers[s, step] = spread
            lo = keep
        ends.append(lo)
    most = max(len(steps) for steps in plans)

    def start_reduce(s, step):
        for copy, _ in reduces[s, step][0]:
            copy.start()

    def advance(step):
        for s in range(STREAMS):
            if step >= len(plans[s]):
                continue
            copies, source, keep, n = reduces[s, step]
            for copy, _ in copies:
                copy.wait()
            value = source[pl.ds(keep, n)]
            for _, buf in copies:
                value = value + buf[...]
            if step + 1 < len(plans[s]):
                acc[pl.ds(keep, n)] = value
                start_reduce(s, step + 1)
            else:
                channels = probe.shape[1]
                res[pl.ds(keep, n)] = probe[pl.ds(keep, n)] + PROBE_STEP * value[:, :channels] / (
                    value[:, channels:] + PROBE_REG
                )
                start_gather(s, step)

    def start_gather(s, step):
        for copy in gathers[s, step]:
            copy.start()

    def back(turn):
        for s in range(STREAMS):
            step = len(plans[s]) - 1 - turn
            if step < 0:
                continue
            for copy in gathers[s, step]:
                copy.wait()
            if step:
                start_gather(s, step - 1)

    for s in range(STREAMS):
        start_reduce(s, 0)
    by_col = Pair(
        "col", cols, gsems, 0,
        (grad.at[:, :, pl.ds(half + tile, half)], colbuf.at[0]),
        (grad.at[:, :, pl.ds(0, half)], colbuf.at[1]),
    )
    by_row = Pair(
        "row", rows, gsems, 2,
        (mid.at[:, pl.ds(half + tile, half)], rowbuf.at[0]),
        (mid.at[:, pl.ds(0, half)], rowbuf.at[1]),
    )
    by_col.start()

    def clear(ref, at):
        def run():
            ref[at] = jnp.zeros_like(ref[at])
        return run

    pl.when(col == 0)(clear(colbuf, 0))
    pl.when(col == cols - 1)(clear(colbuf, 1))
    pl.when(row == 0)(clear(rowbuf, 0))
    pl.when(row == rows - 1)(clear(rowbuf, 1))
    if not last:
        clear_rim(pad, rows, cols, tile, half)

    advance(0)
    weight = weight_of(probe, near, scans, tile)
    by_col.wait()
    mid[...] = grad[:, :, half:half + tile] + colbuf[0] + colbuf[1]
    by_row.start()
    advance(1)
    by_row.wait()
    total = mid[:, half:half + tile] + rowbuf[0] + rowbuf[1]
    new = obj[...] + OBJECT_STEP * total / (weight + OBJECT_REG)
    new_obj[...] = new
    obj_out[...] = new
    if not last:
        halo_row = row_halo(new_obj, pad, hsems, 0, rows, tile, half)
        halo_col = col_halo(pad, hsems, 2, cols, tile, half)
        halo_row.start()
        pad[:, pl.ds(half, tile), pl.ds(half, tile)] = new
    for step in range(2, most):
        advance(step)
    if not last:
        halo_row.wait()
        halo_col.start()
    for turn in range(most):
        back(turn)
    by_col.wait_sent()
    by_row.wait_sent()
    probe_out[...] = res[...]
    if not last:
        halo_col.wait()
        halo_row.wait_sent()
        halo_col.wait_sent()
        pad_out[...] = pad[...]


def exchange(rows, cols, last, scans, obj, probe, near, grad, pgrad):
    tile, full = obj.shape[1], grad.shape[1]
    half = (full - tile) // 2
    channels = grad.shape[0]
    plans = [plan(groups, pgrad.shape[0] // STREAMS) for groups in phases(rows, cols)]
    boxes = sum(n * ((1 << len(group)) - 1) for steps in plans for group, _, n in steps)
    most = max((1 << len(group)) - 1 for steps in plans for group, _, _ in steps)
    longest = max(len(steps) for steps in plans)
    vmem = pl.BlockSpec(memory_space=pltpu.VMEM)
    out_shape = [jax.ShapeDtypeStruct(obj.shape, F32), jax.ShapeDtypeStruct(probe.shape, F32)]
    scratch = [
        pltpu.VMEM((2, channels, full, half), F32),
        pltpu.VMEM((channels, full, tile), F32),
        pltpu.VMEM((2, channels, half, tile), F32),
        pltpu.VMEM(obj.shape, F32),
        pltpu.VMEM(pgrad.shape, F32),
        pltpu.VMEM((boxes,) + pgrad.shape[1:], F32),
        pltpu.VMEM(probe.shape, F32),
        pltpu.SemaphoreType.DMA((2, 4)),
        pltpu.SemaphoreType.DMA((STREAMS, 2, longest, most)),
        pltpu.SemaphoreType.DMA((STREAMS, 2, longest, most)),
    ]
    if not last:
        out_shape.append(jax.ShapeDtypeStruct((2, full, full), F32))
        scratch += [pltpu.VMEM((2, full, full), F32), pltpu.SemaphoreType.DMA((2, 4))]
    return pl.pallas_call(
        lambda *refs: exchange_kernel(rows, cols, last, scans, *refs),
        out_shape=out_shape,
        in_specs=[vmem] * 5,
        out_specs=[vmem] * len(out_shape),
        scratch_shapes=scratch,
        compiler_params=pltpu.CompilerParams(
            collective_id=2 if last else 1,
            has_side_effects=True,
            vmem_limit_bytes=48 * 1024 * 1024,
        ),
    )(obj, probe, near, grad, pgrad)


def split_np(table):
    high = table.astype(np.float32).astype(ml_dtypes.bfloat16)
    low = (table - high.astype(np.float64)).astype(np.float32).astype(ml_dtypes.bfloat16)
    return [high, low]


def tables(side):
    half = side // 2
    n = np.arange(half)[:, None]
    k = np.arange(half)[None, :]
    pieces = []
    for odd in (0, 1):
        angle = 2.0 * math.pi * ((n * (2 * k + odd)) % side) / side
        cos, sin = np.cos(angle) / math.sqrt(side), np.sin(angle) / math.sqrt(side)
        forward = np.block([[cos, -sin], [sin, cos]])
        pieces += split_np(forward) + split_np(forward.T)
    return np.stack(pieces)


def order_table(side):
    half = side // 2
    place = np.concatenate([2 * np.arange(half), 2 * np.arange(half) + 1])
    table = np.zeros((side, side), np.float32)
    table[place, np.arange(side)] = 1.0
    return np.stack([table, table.T]).astype(ml_dtypes.bfloat16)


def split(x):
    high = x.astype(BF16)
    return high, (x - high.astype(F32)).astype(BF16)


def dot(a, b):
    return jnp.dot(a, b, preferred_element_type=F32)


def right(x, tab, at):
    high, low = split(x)
    return dot(high, tab[at]) + (dot(high, tab[at + 1]) + dot(low, tab[at]))


def left(tab, at, x):
    high, low = split(x)
    return dot(tab[at], high) + (dot(tab[at + 1], high) + dot(tab[at], low))


FE, GE, FO, GO = 0, 2, 4, 6


def forward(re, im, tab):
    h = re.shape[1] // 2
    even = right(jnp.concatenate([re[:, :h] + re[:, h:], im[:, :h] + im[:, h:]], 1), tab, FE)
    odd = right(jnp.concatenate([re[:, :h] - re[:, h:], im[:, :h] - im[:, h:]], 1), tab, FO)
    re = jnp.concatenate([even[:, :h], odd[:, :h]], 1)
    im = jnp.concatenate([even[:, h:], odd[:, h:]], 1)
    even = left(tab, GE, jnp.concatenate([re[:h] + re[h:], im[:h] + im[h:]], 0))
    odd = left(tab, GO, jnp.concatenate([re[:h] - re[h:], im[:h] - im[h:]], 0))
    return (
        jnp.concatenate([even[:h], odd[:h]], 0),
        jnp.concatenate([even[h:], odd[h:]], 0),
    )


def inverse(re, im, tab):
    h = re.shape[1] // 2
    even = left(tab, FE, jnp.concatenate([re[:h], im[:h]], 0))
    odd = left(tab, FO, jnp.concatenate([re[h:], im[h:]], 0))
    low, high = even + odd, even - odd
    re = jnp.concatenate([low[:h], high[:h]], 0)
    im = jnp.concatenate([low[h:], high[h:]], 0)
    even = right(jnp.concatenate([re[:, :h], im[:, :h]], 1), tab, GE)
    odd = right(jnp.concatenate([re[:, h:], im[:, h:]], 1), tab, GO)
    low, high = even + odd, even - odd
    return (
        jnp.concatenate([low[:, :h], high[:, :h]], 1),
        jnp.concatenate([low[:, h:], high[:, h:]], 1),
    )


def whole(tiles, at, side):
    blocks = tiles.shape[0] * tiles.shape[2] // side
    per = tiles.shape[0] // blocks
    return jnp.concatenate(
        [tiles[j * per:(j + 1) * per, at].reshape(side, -1) for j in range(blocks)], 1
    )


def put(tiles, at, value, add):
    width = tiles.shape[3]
    per = value.shape[0] // tiles.shape[2]
    for j in range(value.shape[1] // width):
        part = value[:, j * width:(j + 1) * width].reshape(per, tiles.shape[2], width)
        span = slice(j * per, (j + 1) * per)
        tiles[span, at] = tiles[span, at] + part if add else part


def step_kernel(starts, obj, tiles, amp, tab, order, grad, pgrad, wide):
    side = amp.shape[1]
    full = obj.shape[1]
    modes = tiles.shape[1] // 2
    scans = amp.shape[0]
    probe = {(c, k): whole(tiles, c * modes + k, side) for c in range(2) for k in range(modes)}
    wide[...] = jnp.zeros_like(wide)
    for s in range(scans):
        row, col = starts[s, 0] + side // 2, starts[s, 1] + side // 2
        back_row, back_col = lax.rem(full - row, full), lax.rem(full - col, full)
        win = []
        for ch in range(2):
            x = pltpu.roll(obj[ch], back_row, 0)[:side]
            win.append(pltpu.roll(x, back_col, 1)[:, :side])
        wr, wi = win
        ordered = jnp.zeros((side, side), F32)
        for part in split(amp[s]):
            ordered = ordered + dot(order[1], dot(part, order[0]).astype(BF16))
        fars = []
        intensity = jnp.zeros((side, side), F32)
        for k in range(modes):
            pr, pi = probe[0, k], probe[1, k]
            fr, fi = forward(pr * wr - pi * wi, pr * wi + pi * wr, tab)
            intensity = intensity + fr * fr + fi * fi
            fars.append((fr, fi))
        factor = ordered / jnp.maximum(jnp.sqrt(intensity), FLOOR) - 1.0
        gr = jnp.zeros((side, side), F32)
        gi = jnp.zeros((side, side), F32)
        for k in range(modes):
            br, bi = inverse(fars[k][0] * factor, fars[k][1] * factor, tab)
            pr, pi = probe[0, k], probe[1, k]
            gr = gr + pr * br + pi * bi
            gi = gi + pr * bi - pi * br
            for ch, value in enumerate((wr * br + wi * bi, wr * bi - wi * br)):
                at = ch * modes + k
                put(pgrad, at, value, s > 0)
        put(pgrad, 2 * modes, wr * wr + wi * wi, s > 0)
        for ch, value in enumerate((gr, gi)):
            wide[:side, :side] = value
            x = pltpu.roll(pltpu.roll(wide[...], col, 1), row, 0)
            grad[ch] = x if s == 0 else grad[ch] + x


def step(starts, padded, probe, measured, tab, order):
    side = measured.shape[1]
    full = padded.shape[1]
    vmem = pl.BlockSpec(memory_space=pltpu.VMEM)
    flops = 2 * side**3 * 12 * 8
    return pl.pallas_call(
        step_kernel,
        out_shape=(
            jax.ShapeDtypeStruct((2, full, full), F32),
            jax.ShapeDtypeStruct((probe.shape[0], probe.shape[1] + 1) + probe.shape[2:], F32),
        ),
        in_specs=[pl.BlockSpec(memory_space=pltpu.SMEM)] + [vmem] * 5,
        out_specs=(vmem, vmem),
        scratch_shapes=[pltpu.VMEM((full, full), F32)],
        compiler_params=pltpu.CompilerParams(vmem_limit_bytes=48 * 1024 * 1024),
        cost_estimate=pl.CostEstimate(flops=flops, bytes_accessed=6 << 20, transcendentals=0),
    )(starts, padded, probe, measured, tab, order)


def local(object_field, probe, amplitudes, offsets):
    side = probe.shape[2]
    half = side // 2
    rows, cols = lax.axis_size("row"), lax.axis_size("col")
    starts = offsets[0, 0]
    scans = starts.shape[0]
    measured = amplitudes[0, 0]
    tab = jnp.asarray(tables(side))
    order = jnp.asarray(order_table(side))
    channels = probe.shape[0] * probe.shape[1]
    offs = jnp.broadcast_to(starts.reshape(-1, 1), (2 * scans, 128))
    modes = probe.reshape(channels, side, side)
    padded, near, tiles = halo(rows, cols, object_field, offs, modes, half)
    for iteration in range(ITERS):
        last = iteration + 1 == ITERS
        grad, pgrad = step(starts, padded, tiles, measured, tab, order)
        out = exchange(rows, cols, last, scans, object_field, tiles, near, grad, pgrad)
        object_field, tiles = out[:2]
        if not last:
            padded = out[2]
    back = tiles.reshape(side // 128, side // 8, channels, 8, 128).transpose(2, 1, 3, 0, 4)
    return object_field, back.reshape(probe.shape)


def solution(mesh):
    return jax.shard_map(
        local,
        mesh=mesh,
        in_specs=(
            P(None, "row", "col"),
            P(),
            P("row", "col", None, None, None),
            P("row", "col", None, None),
        ),
        out_specs=(P(None, "row", "col"), P()),
        check_vma=False,
    )
```

```python
import math

import jax
import jax.numpy as jnp
import numpy as np
import ml_dtypes
from jax import lax
from jax.experimental import pallas as pl
from jax.experimental.pallas import tpu as pltpu
from jax.sharding import PartitionSpec as P

ITERS = 2
FLOOR = 0.5
OBJECT_STEP = 0.5
OBJECT_REG = 0.5
PROBE_STEP = 1.0
PROBE_REG = 1.0
F32 = jnp.float32
BF16 = jnp.bfloat16
STREAMS = 2
ABSENT = 1 << 20


MESH = pl.DeviceIdType.MESH


def bits_of(axis, count):
    return [(axis, b) for b in range(count.bit_length() - 1)]


def phases(rows, cols):
    row_bits, col_bits = bits_of("row", rows), bits_of("col", cols)
    rest = row_bits[1:] + col_bits[2:]
    groups = [col_bits[:1], col_bits[1:2] + row_bits[:1]]
    return groups + [rest[i:i + 2] for i in range(0, len(rest), 2)]


def plan(groups, count):
    steps = []
    for group in groups:
        if count % (1 << len(group)) == 0:
            count //= 1 << len(group)
            steps.append((group, True, count))
        else:
            steps += [([bit], False, count) for bit in group]
    return steps


def peer(group, mask):
    device, mine, theirs = {}, 0, 0
    for i, (axis, bit) in enumerate(group):
        me = lax.axis_index(axis)
        held = lax.rem(me // (1 << bit), 2)
        mine = mine + held * (1 << i)
        if mask >> i & 1:
            device[axis] = device.get(axis, me) + (1 << bit) * (1 - 2 * held)
            theirs = theirs + (1 - held) * (1 << i)
        else:
            theirs = theirs + held * (1 << i)
    return device, mine, theirs


def remote(src, dst, sems, at, device):
    return pltpu.make_async_remote_copy(
        src_ref=src, dst_ref=dst, send_sem=sems.at[(0,) + at], recv_sem=sems.at[(1,) + at],
        device_id=device, device_id_type=MESH,
    )


def greet(rows, cols, groups):
    barrier = pltpu.get_barrier_semaphore()
    row, col = lax.axis_index("row"), lax.axis_index("col")
    devices = [
        {"row": lax.rem(row + 1, rows)}, {"row": lax.rem(row + rows - 1, rows)},
        {"col": lax.rem(col + 1, cols)}, {"col": lax.rem(col + cols - 1, cols)},
    ]
    for group in groups:
        devices += [peer(group, mask)[0] for mask in range(1, 1 << len(group))]
    for device in devices:
        pl.semaphore_signal(barrier, inc=1, device_id=device, device_id_type=MESH)
    pl.semaphore_wait(barrier, len(devices))


class Pair:
    def __init__(self, axis, count, sems, at, up, down):
        me = lax.axis_index(axis)
        self.not_last, self.not_first = me < count - 1, me > 0
        self.up = remote(up[0], up[1], sems, (at,), {axis: jnp.minimum(me + 1, count - 1)})
        self.down = remote(down[0], down[1], sems, (at + 1,), {axis: jnp.maximum(me - 1, 0)})

    def start(self):
        pl.when(self.not_last)(self.up.start)
        pl.when(self.not_first)(self.down.start)

    def wait(self):
        pl.when(self.not_first)(self.up.wait_recv)
        pl.when(self.not_last)(self.down.wait_recv)

    def wait_sent(self):
        pl.when(self.not_last)(self.up.wait_send)
        pl.when(self.not_first)(self.down.wait_send)


def row_halo(tile_ref, pad, sems, at, rows, tile, half):
    own = pl.ds(half, tile)
    return Pair(
        "row", rows, sems, at,
        (tile_ref, pad.at[:, pl.ds(0, half), own]),
        (tile_ref, pad.at[:, pl.ds(half + tile, half), own]),
    )


def col_halo(pad, sems, at, cols, tile, half):
    own = pl.ds(half, tile)
    return Pair(
        "col", cols, sems, at,
        (pad.at[:, :, own], pad.at[:, :, pl.ds(0, half)]),
        (pad.at[:, :, own], pad.at[:, :, pl.ds(half + tile, half)]),
    )


def clear_rim(pad, rows, cols, tile, half):
    row, col = lax.axis_index("row"), lax.axis_index("col")
    own = pl.ds(half, tile)

    def clear(*where):
        def run():
            pad[where] = jnp.zeros_like(pad[where])
        return run

    every = slice(None)
    pl.when(row == 0)(clear(every, pl.ds(0, half), own))
    pl.when(row == rows - 1)(clear(every, pl.ds(half + tile, half), own))
    pl.when(col == 0)(clear(every, every, pl.ds(0, half)))
    pl.when(col == cols - 1)(clear(every, every, pl.ds(half + tile, half)))


def halo_kernel(rows, cols, obj, offs, out, near_out, pad, near, sems):
    tile = obj.shape[1]
    half = (pad.shape[1] - tile) // 2
    greet(rows, cols, ())
    by_row = row_halo(obj, pad, sems, 0, rows, tile, half)
    by_row.start()
    offs_row = Pair("row", rows, sems, 4, (offs, near.at[1, 0]), (offs, near.at[1, 2]))
    offs_row.start()
    near[1, 1] = offs[...]
    row, col = lax.axis_index("row"), lax.axis_index("col")

    def absent(*where):
        def run():
            near[where] = jnp.full_like(near[where], ABSENT)
        return run

    pl.when(row == 0)(absent(1, 0))
    pl.when(row == rows - 1)(absent(1, 2))
    pl.when(col == 0)(absent(0))
    pl.when(col == cols - 1)(absent(2))
    clear_rim(pad, rows, cols, tile, half)
    pad[:, pl.ds(half, tile), pl.ds(half, tile)] = obj[...]
    by_row.wait()
    by_col = col_halo(pad, sems, 2, cols, tile, half)
    by_col.start()
    offs_row.wait()
    offs_col = Pair("col", cols, sems, 6, (near.at[1], near.at[0]), (near.at[1], near.at[2]))
    offs_col.start()
    by_col.wait()
    offs_col.wait()
    for pair in (by_row, by_col, offs_row, offs_col):
        pair.wait_sent()
    out[...] = pad[...]
    near_out[...] = near[...]


def halo(rows, cols, obj, offs, half):
    full = obj.shape[1] + 2 * half
    vmem = pl.BlockSpec(memory_space=pltpu.VMEM)
    return pl.pallas_call(
        lambda *refs: halo_kernel(rows, cols, *refs),
        out_shape=(
            jax.ShapeDtypeStruct((2, full, full), F32),
            jax.ShapeDtypeStruct((3, 3) + offs.shape, jnp.int32),
        ),
        in_specs=[vmem, vmem],
        out_specs=(vmem, vmem),
        scratch_shapes=[
            pltpu.VMEM((2, full, full), F32),
            pltpu.VMEM((3, 3) + offs.shape, jnp.int32),
            pltpu.SemaphoreType.DMA((2, 8)),
        ],
        compiler_params=pltpu.CompilerParams(
            collective_id=0, has_side_effects=True, vmem_limit_bytes=32 * 1024 * 1024
        ),
    )(obj, offs)


def weight_of(probe, near, scans, tile):
    channels = probe.shape[1]
    power = probe[:, 0] * probe[:, 0]
    for at in range(1, channels):
        power = power + probe[:, at] * probe[:, at]
    side = math.isqrt(power.size)
    power = whole(power[:, None], 0, side)
    both = jnp.concatenate(split(power), 1)
    along = lax.broadcasted_iota(jnp.int32, (tile, side), 0) - lax.broadcasted_iota(
        jnp.int32, (tile, side), 1
    )
    across = lax.broadcasted_iota(jnp.int32, (side, tile), 1) - lax.broadcasted_iota(
        jnp.int32, (side, tile), 0
    )
    weight = jnp.zeros((tile, tile), F32)
    for dc in range(3):
        for dr in range(3):
            for s in range(scans):
                top = near[dc, dr, 2 * s:2 * s + 1, :] + (dr - 1) * tile
                edge = near[dc, dr, 2 * s + 1:2 * s + 2, :] + (dc - 1) * tile
                top = jnp.concatenate([top] * (side // top.shape[1]), 1)
                pick = jnp.where(along == top, 1.0, 0.0).astype(BF16)
                place = jnp.where(across == edge, 1.0, 0.0).astype(BF16)
                cut = dot(pick, both)
                high, low = split(cut[:, :side] + cut[:, side:])
                weight = weight + (dot(high, place) + dot(low, place))
    return weight


def exchange_kernel(rows, cols, last, scans, obj, probe, near, grad, pgrad, *refs):
    if last:
        obj_out, probe_out, colbuf, mid, rowbuf, new_obj, acc, inbox, res, gsems, rsems, asems = refs
    else:
        (obj_out, probe_out, pad_out, colbuf, mid, rowbuf, new_obj, acc, inbox, res,
         gsems, rsems, asems, pad, hsems) = refs
    tile = obj.shape[1]
    full = grad.shape[1]
    half = (full - tile) // 2
    row, col = lax.axis_index("row"), lax.axis_index("col")
    groups = phases(rows, cols)
    greet(rows, cols, groups)
    spots = pgrad.shape[0] // STREAMS
    steps = plan(groups, spots)
    box = 0
    reduces, gathers, ends = {}, {}, []
    for s in range(STREAMS):
        lo = s * spots
        for step, (group, scatters, n) in enumerate(steps):
            source = pgrad if step == 0 else acc
            _, mine, _ = peer(group, 0)
            keep = lo + mine * n if scatters else lo
            copies, spread = [], []
            for mask in range(1, 1 << len(group)):
                device, _, theirs = peer(group, mask)
                send = lo + theirs * n if scatters else lo
                buf = inbox.at[pl.ds(box, n)]
                box += n
                at = (step, mask - 1)
                copies.append((remote(source.at[pl.ds(send, n)], buf, rsems.at[s], at, device), buf))
                if scatters:
                    span = res.at[pl.ds(keep, n)]
                    spread.append(remote(span, span, asems.at[s], at, device))
            reduces[s, step] = (copies, source, keep, n)
            gathers[s, step] = spread
            lo = keep
        ends.append(lo)
    total_steps = len(steps)

    def start_reduce(s, step):
        for copy, _ in reduces[s, step][0]:
            copy.start()

    def advance(step):
        for s in range(STREAMS):
            copies, source, keep, n = reduces[s, step]
            for copy, _ in copies:
                copy.wait()
            value = source[pl.ds(keep, n)]
            for _, buf in copies:
                value = value + buf[...]
            if step + 1 < total_steps:
                acc[pl.ds(keep, n)] = value
                start_reduce(s, step + 1)
            else:
                channels = probe.shape[1]
                res[pl.ds(keep, n)] = probe[pl.ds(keep, n)] + PROBE_STEP * value[:, :channels] / (
                    value[:, channels:] + PROBE_REG
                )
                start_gather(s, step)

    def start_gather(s, step):
        for copy in gathers[s, step]:
            copy.start()

    def back(step):
        for s in range(STREAMS):
            for copy in gathers[s, step]:
                copy.wait()
            if step:
                start_gather(s, step - 1)

    by_col = Pair(
        "col", cols, gsems, 0,
        (grad.at[:, :, pl.ds(half + tile, half)], colbuf.at[0]),
        (grad.at[:, :, pl.ds(0, half)], colbuf.at[1]),
    )
    by_row = Pair(
        "row", rows, gsems, 2,
        (mid.at[:, pl.ds(half + tile, half)], rowbuf.at[0]),
        (mid.at[:, pl.ds(0, half)], rowbuf.at[1]),
    )
    by_col.start()
    for s in range(STREAMS):
        start_reduce(s, 0)

    def clear(ref, at):
        def run():
            ref[at] = jnp.zeros_like(ref[at])
        return run

    pl.when(col == 0)(clear(colbuf, 0))
    pl.when(col == cols - 1)(clear(colbuf, 1))
    pl.when(row == 0)(clear(rowbuf, 0))
    pl.when(row == rows - 1)(clear(rowbuf, 1))
    if not last:
        clear_rim(pad, rows, cols, tile, half)

    advance(0)
    by_col.wait()
    mid[...] = grad[:, :, half:half + tile] + colbuf[0] + colbuf[1]
    by_row.start()
    weight = weight_of(probe, near, scans, tile)
    advance(1)
    by_row.wait()
    total = mid[:, half:half + tile] + rowbuf[0] + rowbuf[1]
    new = obj[...] + OBJECT_STEP * total / (weight + OBJECT_REG)
    new_obj[...] = new
    obj_out[...] = new
    if not last:
        halo_row = row_halo(new_obj, pad, hsems, 0, rows, tile, half)
        halo_col = col_halo(pad, hsems, 2, cols, tile, half)
        halo_row.start()
        pad[:, pl.ds(half, tile), pl.ds(half, tile)] = new
    for step in range(2, total_steps):
        advance(step)
    if not last:
        halo_row.wait()
        halo_col.start()
    for step in reversed(range(total_steps)):
        back(step)
    by_col.wait_sent()
    by_row.wait_sent()
    probe_out[...] = res[...]
    if not last:
        halo_col.wait()
        halo_row.wait_sent()
        halo_col.wait_sent()
        pad_out[...] = pad[...]


def exchange(rows, cols, last, scans, obj, probe, near, grad, pgrad):
    tile, full = obj.shape[1], grad.shape[1]
    half = (full - tile) // 2
    channels = grad.shape[0]
    steps = plan(phases(rows, cols), pgrad.shape[0] // STREAMS)
    boxes = STREAMS * sum(n * ((1 << len(group)) - 1) for group, _, n in steps)
    most = max((1 << len(group)) - 1 for group, _, _ in steps)
    vmem = pl.BlockSpec(memory_space=pltpu.VMEM)
    out_shape = [jax.ShapeDtypeStruct(obj.shape, F32), jax.ShapeDtypeStruct(probe.shape, F32)]
    scratch = [
        pltpu.VMEM((2, channels, full, half), F32),
        pltpu.VMEM((channels, full, tile), F32),
        pltpu.VMEM((2, channels, half, tile), F32),
        pltpu.VMEM(obj.shape, F32),
        pltpu.VMEM(pgrad.shape, F32),
        pltpu.VMEM((boxes,) + pgrad.shape[1:], F32),
        pltpu.VMEM(probe.shape, F32),
        pltpu.SemaphoreType.DMA((2, 4)),
        pltpu.SemaphoreType.DMA((STREAMS, 2, len(steps), most)),
        pltpu.SemaphoreType.DMA((STREAMS, 2, len(steps), most)),
    ]
    if not last:
        out_shape.append(jax.ShapeDtypeStruct((2, full, full), F32))
        scratch += [pltpu.VMEM((2, full, full), F32), pltpu.SemaphoreType.DMA((2, 4))]
    return pl.pallas_call(
        lambda *refs: exchange_kernel(rows, cols, last, scans, *refs),
        out_shape=out_shape,
        in_specs=[vmem] * 5,
        out_specs=[vmem] * len(out_shape),
        scratch_shapes=scratch,
        compiler_params=pltpu.CompilerParams(
            collective_id=2 if last else 1,
            has_side_effects=True,
            vmem_limit_bytes=48 * 1024 * 1024,
        ),
    )(obj, probe, near, grad, pgrad)


def split_np(table):
    high = table.astype(np.float32).astype(ml_dtypes.bfloat16)
    low = (table - high.astype(np.float64)).astype(np.float32).astype(ml_dtypes.bfloat16)
    return [high, low]


def tables(side):
    half = side // 2
    n = np.arange(half)[:, None]
    k = np.arange(half)[None, :]
    pieces = []
    for odd in (0, 1):
        angle = 2.0 * math.pi * ((n * (2 * k + odd)) % side) / side
        cos, sin = np.cos(angle) / math.sqrt(side), np.sin(angle) / math.sqrt(side)
        forward = np.block([[cos, -sin], [sin, cos]])
        pieces += split_np(forward) + split_np(forward.T)
    return np.stack(pieces)


def order_table(side):
    half = side // 2
    place = np.concatenate([2 * np.arange(half), 2 * np.arange(half) + 1])
    table = np.zeros((side, side), np.float32)
    table[place, np.arange(side)] = 1.0
    return np.stack([table, table.T]).astype(ml_dtypes.bfloat16)


def split(x):
    high = x.astype(BF16)
    return high, (x - high.astype(F32)).astype(BF16)


def dot(a, b):
    return jnp.dot(a, b, preferred_element_type=F32)


def right(x, tab, at):
    high, low = split(x)
    return dot(high, tab[at]) + (dot(high, tab[at + 1]) + dot(low, tab[at]))


def left(tab, at, x):
    high, low = split(x)
    return dot(tab[at], high) + (dot(tab[at + 1], high) + dot(tab[at], low))


FE, GE, FO, GO = 0, 2, 4, 6


def forward(re, im, tab):
    h = re.shape[1] // 2
    even = right(jnp.concatenate([re[:, :h] + re[:, h:], im[:, :h] + im[:, h:]], 1), tab, FE)
    odd = right(jnp.concatenate([re[:, :h] - re[:, h:], im[:, :h] - im[:, h:]], 1), tab, FO)
    re = jnp.concatenate([even[:, :h], odd[:, :h]], 1)
    im = jnp.concatenate([even[:, h:], odd[:, h:]], 1)
    even = left(tab, GE, jnp.concatenate([re[:h] + re[h:], im[:h] + im[h:]], 0))
    odd = left(tab, GO, jnp.concatenate([re[:h] - re[h:], im[:h] - im[h:]], 0))
    return (
        jnp.concatenate([even[:h], odd[:h]], 0),
        jnp.concatenate([even[h:], odd[h:]], 0),
    )


def inverse(re, im, tab):
    h = re.shape[1] // 2
    even = left(tab, FE, jnp.concatenate([re[:h], im[:h]], 0))
    odd = left(tab, FO, jnp.concatenate([re[h:], im[h:]], 0))
    low, high = even + odd, even - odd
    re = jnp.concatenate([low[:h], high[:h]], 0)
    im = jnp.concatenate([low[h:], high[h:]], 0)
    even = right(jnp.concatenate([re[:, :h], im[:, :h]], 1), tab, GE)
    odd = right(jnp.concatenate([re[:, h:], im[:, h:]], 1), tab, GO)
    low, high = even + odd, even - odd
    return (
        jnp.concatenate([low[:, :h], high[:, :h]], 1),
        jnp.concatenate([low[:, h:], high[:, h:]], 1),
    )


def whole(tiles, at, side):
    blocks = tiles.shape[0] * tiles.shape[2] // side
    per = tiles.shape[0] // blocks
    return jnp.concatenate(
        [tiles[j * per:(j + 1) * per, at].reshape(side, -1) for j in range(blocks)], 1
    )


def put(tiles, at, value, add):
    width = tiles.shape[3]
    per = value.shape[0] // tiles.shape[2]
    for j in range(value.shape[1] // width):
        part = value[:, j * width:(j + 1) * width].reshape(per, tiles.shape[2], width)
        span = slice(j * per, (j + 1) * per)
        tiles[span, at] = tiles[span, at] + part if add else part


def step_kernel(starts, obj, tiles, amp, tab, order, grad, pgrad, wide):
    side = amp.shape[1]
    full = obj.shape[1]
    modes = tiles.shape[1] // 2
    scans = amp.shape[0]
    probe = {(c, k): whole(tiles, c * modes + k, side) for c in range(2) for k in range(modes)}
    wide[...] = jnp.zeros_like(wide)
    for s in range(scans):
        row, col = starts[s, 0] + side // 2, starts[s, 1] + side // 2
        back_row, back_col = lax.rem(full - row, full), lax.rem(full - col, full)
        win = []
        for ch in range(2):
            x = pltpu.roll(obj[ch], back_row, 0)[:side]
            win.append(pltpu.roll(x, back_col, 1)[:, :side])
        wr, wi = win
        ordered = jnp.zeros((side, side), F32)
        for part in split(amp[s]):
            ordered = ordered + dot(order[1], dot(part, order[0]).astype(BF16))
        fars = []
        intensity = jnp.zeros((side, side), F32)
        for k in range(modes):
            pr, pi = probe[0, k], probe[1, k]
            fr, fi = forward(pr * wr - pi * wi, pr * wi + pi * wr, tab)
            intensity = intensity + fr * fr + fi * fi
            fars.append((fr, fi))
        factor = ordered / jnp.maximum(jnp.sqrt(intensity), FLOOR) - 1.0
        gr = jnp.zeros((side, side), F32)
        gi = jnp.zeros((side, side), F32)
        for k in range(modes):
            br, bi = inverse(fars[k][0] * factor, fars[k][1] * factor, tab)
            pr, pi = probe[0, k], probe[1, k]
            gr = gr + pr * br + pi * bi
            gi = gi + pr * bi - pi * br
            for ch, value in enumerate((wr * br + wi * bi, wr * bi - wi * br)):
                at = ch * modes + k
                put(pgrad, at, value, s > 0)
        put(pgrad, 2 * modes, wr * wr + wi * wi, s > 0)
        for ch, value in enumerate((gr, gi)):
            wide[:side, :side] = value
            x = pltpu.roll(pltpu.roll(wide[...], col, 1), row, 0)
            grad[ch] = x if s == 0 else grad[ch] + x


def step(starts, padded, probe, measured, tab, order):
    side = measured.shape[1]
    full = padded.shape[1]
    vmem = pl.BlockSpec(memory_space=pltpu.VMEM)
    flops = 2 * side**3 * 12 * 8
    return pl.pallas_call(
        step_kernel,
        out_shape=(
            jax.ShapeDtypeStruct((2, full, full), F32),
            jax.ShapeDtypeStruct((probe.shape[0], probe.shape[1] + 1) + probe.shape[2:], F32),
        ),
        in_specs=[pl.BlockSpec(memory_space=pltpu.SMEM)] + [vmem] * 5,
        out_specs=(vmem, vmem),
        scratch_shapes=[pltpu.VMEM((full, full), F32)],
        compiler_params=pltpu.CompilerParams(vmem_limit_bytes=48 * 1024 * 1024),
        cost_estimate=pl.CostEstimate(flops=flops, bytes_accessed=6 << 20, transcendentals=0),
    )(starts, padded, probe, measured, tab, order)


def local(object_field, probe, amplitudes, offsets):
    side = probe.shape[2]
    half = side // 2
    rows, cols = lax.axis_size("row"), lax.axis_size("col")
    starts = offsets[0, 0]
    scans = starts.shape[0]
    measured = amplitudes[0, 0]
    tab = jnp.asarray(tables(side))
    order = jnp.asarray(order_table(side))
    channels = probe.shape[0] * probe.shape[1]
    cut = (channels, side // 8, 8, side // 128, 128)
    tiles = probe.reshape(cut).transpose(3, 1, 0, 2, 4).reshape(-1, channels, 8, 128)
    offs = jnp.broadcast_to(starts.reshape(-1, 1), (2 * scans, 128))
    padded, near = halo(rows, cols, object_field, offs, half)
    for iteration in range(ITERS):
        last = iteration + 1 == ITERS
        grad, pgrad = step(starts, padded, tiles, measured, tab, order)
        out = exchange(rows, cols, last, scans, object_field, tiles, near, grad, pgrad)
        object_field, tiles = out[:2]
        if not last:
            padded = out[2]
    back = tiles.reshape(side // 128, side // 8, channels, 8, 128).transpose(2, 1, 3, 0, 4)
    return object_field, back.reshape(probe.shape)


def solution(mesh):
    return jax.shard_map(
        local,
        mesh=mesh,
        in_specs=(
            P(None, "row", "col"),
            P(),
            P("row", "col", None, None, None),
            P("row", "col", None, None),
        ),
        out_specs=(P(None, "row", "col"), P()),
        check_vma=False,
    )
```

```python
import math

import jax
import jax.numpy as jnp
import numpy as np
import ml_dtypes
from jax import lax
from jax.experimental import pallas as pl
from jax.experimental.pallas import tpu as pltpu
from jax.sharding import PartitionSpec as P

ITERS = 2
FLOOR = 0.5
OBJECT_STEP = 0.5
OBJECT_REG = 0.5
PROBE_STEP = 1.0
PROBE_REG = 1.0
F32 = jnp.float32
BF16 = jnp.bfloat16
STREAMS = 2
ABSENT = 1 << 20


MESH = pl.DeviceIdType.MESH


def bits_of(axis, count):
    return [(axis, b) for b in range(count.bit_length() - 1)]


def phases(rows, cols):
    row_bits, col_bits = bits_of("row", rows), bits_of("col", cols)
    rest = row_bits[1:] + col_bits[2:]
    groups = [col_bits[:1], col_bits[1:2] + row_bits[:1]]
    return groups + [rest[i:i + 2] for i in range(0, len(rest), 2)]


def plan(groups, count):
    steps = []
    for group in groups:
        if count % (1 << len(group)) == 0:
            count //= 1 << len(group)
            steps.append((group, True, count))
        else:
            steps += [([bit], False, count) for bit in group]
    return steps


def peer(group, mask):
    device, mine, theirs = {}, 0, 0
    for i, (axis, bit) in enumerate(group):
        me = lax.axis_index(axis)
        held = lax.rem(me // (1 << bit), 2)
        mine = mine + held * (1 << i)
        if mask >> i & 1:
            device[axis] = device.get(axis, me) + (1 << bit) * (1 - 2 * held)
            theirs = theirs + (1 - held) * (1 << i)
        else:
            theirs = theirs + held * (1 << i)
    return device, mine, theirs


def remote(src, dst, sems, at, device):
    return pltpu.make_async_remote_copy(
        src_ref=src, dst_ref=dst, send_sem=sems.at[(0,) + at], recv_sem=sems.at[(1,) + at],
        device_id=device, device_id_type=MESH,
    )


def greet(rows, cols, groups):
    barrier = pltpu.get_barrier_semaphore()
    row, col = lax.axis_index("row"), lax.axis_index("col")
    devices = [
        {"row": lax.rem(row + 1, rows)}, {"row": lax.rem(row + rows - 1, rows)},
        {"col": lax.rem(col + 1, cols)}, {"col": lax.rem(col + cols - 1, cols)},
    ]
    for group in groups:
        devices += [peer(group, mask)[0] for mask in range(1, 1 << len(group))]
    for device in devices:
        pl.semaphore_signal(barrier, inc=1, device_id=device, device_id_type=MESH)
    pl.semaphore_wait(barrier, len(devices))


class Pair:
    def __init__(self, axis, count, sems, at, up, down):
        me = lax.axis_index(axis)
        self.not_last, self.not_first = me < count - 1, me > 0
        self.up = remote(up[0], up[1], sems, (at,), {axis: jnp.minimum(me + 1, count - 1)})
        self.down = remote(down[0], down[1], sems, (at + 1,), {axis: jnp.maximum(me - 1, 0)})

    def start(self):
        pl.when(self.not_last)(self.up.start)
        pl.when(self.not_first)(self.down.start)

    def wait(self):
        pl.when(self.not_first)(self.up.wait_recv)
        pl.when(self.not_last)(self.down.wait_recv)

    def wait_sent(self):
        pl.when(self.not_last)(self.up.wait_send)
        pl.when(self.not_first)(self.down.wait_send)


def row_halo(tile_ref, pad, sems, at, rows, tile, half):
    own = pl.ds(half, tile)
    return Pair(
        "row", rows, sems, at,
        (tile_ref, pad.at[:, pl.ds(0, half), own]),
        (tile_ref, pad.at[:, pl.ds(half + tile, half), own]),
    )


def col_halo(pad, sems, at, cols, tile, half):
    own = pl.ds(half, tile)
    return Pair(
        "col", cols, sems, at,
        (pad.at[:, :, own], pad.at[:, :, pl.ds(0, half)]),
        (pad.at[:, :, own], pad.at[:, :, pl.ds(half + tile, half)]),
    )


def clear_rim(pad, rows, cols, tile, half):
    row, col = lax.axis_index("row"), lax.axis_index("col")
    own = pl.ds(half, tile)

    def clear(*where):
        def run():
            pad[where] = jnp.zeros_like(pad[where])
        return run

    every = slice(None)
    pl.when(row == 0)(clear(every, pl.ds(0, half), own))
    pl.when(row == rows - 1)(clear(every, pl.ds(half + tile, half), own))
    pl.when(col == 0)(clear(every, every, pl.ds(0, half)))
    pl.when(col == cols - 1)(clear(every, every, pl.ds(half + tile, half)))


def halo_kernel(rows, cols, obj, offs, out, near_out, pad, near, sems):
    tile = obj.shape[1]
    half = (pad.shape[1] - tile) // 2
    greet(rows, cols, ())
    by_row = row_halo(obj, pad, sems, 0, rows, tile, half)
    by_row.start()
    offs_row = Pair("row", rows, sems, 4, (offs, near.at[1, 0]), (offs, near.at[1, 2]))
    offs_row.start()
    near[1, 1] = offs[...]
    row, col = lax.axis_index("row"), lax.axis_index("col")

    def absent(*where):
        def run():
            near[where] = jnp.full_like(near[where], ABSENT)
        return run

    pl.when(row == 0)(absent(1, 0))
    pl.when(row == rows - 1)(absent(1, 2))
    pl.when(col == 0)(absent(0))
    pl.when(col == cols - 1)(absent(2))
    clear_rim(pad, rows, cols, tile, half)
    pad[:, pl.ds(half, tile), pl.ds(half, tile)] = obj[...]
    by_row.wait()
    by_col = col_halo(pad, sems, 2, cols, tile, half)
    by_col.start()
    offs_row.wait()
    offs_col = Pair("col", cols, sems, 6, (near.at[1], near.at[0]), (near.at[1], near.at[2]))
    offs_col.start()
    by_col.wait()
    offs_col.wait()
    for pair in (by_row, by_col, offs_row, offs_col):
        pair.wait_sent()
    out[...] = pad[...]
    near_out[...] = near[...]


def halo(rows, cols, obj, offs, half):
    full = obj.shape[1] + 2 * half
    vmem = pl.BlockSpec(memory_space=pltpu.VMEM)
    return pl.pallas_call(
        lambda *refs: halo_kernel(rows, cols, *refs),
        out_shape=(
            jax.ShapeDtypeStruct((2, full, full), F32),
            jax.ShapeDtypeStruct((3, 3) + offs.shape, jnp.int32),
        ),
        in_specs=[vmem, vmem],
        out_specs=(vmem, vmem),
        scratch_shapes=[
            pltpu.VMEM((2, full, full), F32),
            pltpu.VMEM((3, 3) + offs.shape, jnp.int32),
            pltpu.SemaphoreType.DMA((2, 8)),
        ],
        compiler_params=pltpu.CompilerParams(
            collective_id=0, has_side_effects=True, vmem_limit_bytes=32 * 1024 * 1024
        ),
    )(obj, offs)


def weight_of(probe, near, scans, tile):
    channels = probe.shape[1]
    power = probe[:, 0] * probe[:, 0]
    for at in range(1, channels):
        power = power + probe[:, at] * probe[:, at]
    side = math.isqrt(power.size)
    power = whole(power[:, None], 0, side)
    both = jnp.concatenate(split(power), 1)
    along = lax.broadcasted_iota(jnp.int32, (tile, side), 0) - lax.broadcasted_iota(
        jnp.int32, (tile, side), 1
    )
    across = lax.broadcasted_iota(jnp.int32, (side, tile), 1) - lax.broadcasted_iota(
        jnp.int32, (side, tile), 0
    )
    weight = jnp.zeros((tile, tile), F32)
    for dc in range(3):
        for dr in range(3):
            for s in range(scans):
                top = near[dc, dr, 2 * s:2 * s + 1, :] + (dr - 1) * tile
                edge = near[dc, dr, 2 * s + 1:2 * s + 2, :] + (dc - 1) * tile
                top = jnp.concatenate([top] * (side // top.shape[1]), 1)
                pick = jnp.where(along == top, 1.0, 0.0).astype(BF16)
                place = jnp.where(across == edge, 1.0, 0.0).astype(BF16)
                cut = dot(pick, both)
                high, low = split(cut[:, :side] + cut[:, side:])
                weight = weight + (dot(high, place) + dot(low, place))
    return weight


def exchange_kernel(rows, cols, last, scans, obj, probe, near, grad, pgrad, *refs):
    if last:
        obj_out, probe_out, colbuf, mid, rowbuf, new_obj, acc, inbox, res, gsems, rsems, asems = refs
    else:
        (obj_out, probe_out, pad_out, colbuf, mid, rowbuf, new_obj, acc, inbox, res,
         gsems, rsems, asems, pad, hsems) = refs
    tile = obj.shape[1]
    full = grad.shape[1]
    half = (full - tile) // 2
    row, col = lax.axis_index("row"), lax.axis_index("col")
    groups = phases(rows, cols)
    greet(rows, cols, groups)
    spots = pgrad.shape[0] // STREAMS
    steps = plan(groups, spots)
    box = 0
    reduces, gathers, ends = {}, {}, []
    for s in range(STREAMS):
        lo = s * spots
        for step, (group, scatters, n) in enumerate(steps):
            source = pgrad if step == 0 else acc
            _, mine, _ = peer(group, 0)
            keep = lo + mine * n if scatters else lo
            copies, spread = [], []
            for mask in range(1, 1 << len(group)):
                device, _, theirs = peer(group, mask)
                send = lo + theirs * n if scatters else lo
                buf = inbox.at[pl.ds(box, n)]
                box += n
                at = (step, mask - 1)
                copies.append((remote(source.at[pl.ds(send, n)], buf, rsems.at[s], at, device), buf))
                if scatters:
                    span = res.at[pl.ds(keep, n)]
                    spread.append(remote(span, span, asems.at[s], at, device))
            reduces[s, step] = (copies, source, keep, n)
            gathers[s, step] = spread
            lo = keep
        ends.append(lo)
    total_steps = len(steps)

    def start_reduce(s, step):
        for copy, _ in reduces[s, step][0]:
            copy.start()

    def advance(step):
        for s in range(STREAMS):
            copies, source, keep, n = reduces[s, step]
            for copy, _ in copies:
                copy.wait()
            value = source[pl.ds(keep, n)]
            for _, buf in copies:
                value = value + buf[...]
            if step + 1 < total_steps:
                acc[pl.ds(keep, n)] = value
                start_reduce(s, step + 1)
            else:
                channels = probe.shape[1]
                res[pl.ds(keep, n)] = probe[pl.ds(keep, n)] + PROBE_STEP * value[:, :channels] / (
                    value[:, channels:] + PROBE_REG
                )
                start_gather(s, step)

    def start_gather(s, step):
        for copy in gathers[s, step]:
            copy.start()

    def back(step):
        for s in range(STREAMS):
            for copy in gathers[s, step]:
                copy.wait()
            if step:
                start_gather(s, step - 1)

    for s in range(STREAMS):
        start_reduce(s, 0)
    by_col = Pair(
        "col", cols, gsems, 0,
        (grad.at[:, :, pl.ds(half + tile, half)], colbuf.at[0]),
        (grad.at[:, :, pl.ds(0, half)], colbuf.at[1]),
    )
    by_row = Pair(
        "row", rows, gsems, 2,
        (mid.at[:, pl.ds(half + tile, half)], rowbuf.at[0]),
        (mid.at[:, pl.ds(0, half)], rowbuf.at[1]),
    )
    by_col.start()

    def clear(ref, at):
        def run():
            ref[at] = jnp.zeros_like(ref[at])
        return run

    pl.when(col == 0)(clear(colbuf, 0))
    pl.when(col == cols - 1)(clear(colbuf, 1))
    pl.when(row == 0)(clear(rowbuf, 0))
    pl.when(row == rows - 1)(clear(rowbuf, 1))
    if not last:
        clear_rim(pad, rows, cols, tile, half)

    advance(0)
    weight = weight_of(probe, near, scans, tile)
    by_col.wait()
    mid[...] = grad[:, :, half:half + tile] + colbuf[0] + colbuf[1]
    by_row.start()
    if last:
        advance(1)
    by_row.wait()
    total = mid[:, half:half + tile] + rowbuf[0] + rowbuf[1]
    new = obj[...] + OBJECT_STEP * total / (weight + OBJECT_REG)
    new_obj[...] = new
    obj_out[...] = new
    if not last:
        halo_row = row_halo(new_obj, pad, hsems, 0, rows, tile, half)
        halo_col = col_halo(pad, hsems, 2, cols, tile, half)
        halo_row.start()
        pad[:, pl.ds(half, tile), pl.ds(half, tile)] = new
        advance(1)
        halo_row.wait()
        halo_col.start()
    for step in range(2, total_steps):
        advance(step)
    for step in reversed(range(total_steps)):
        back(step)
    by_col.wait_sent()
    by_row.wait_sent()
    probe_out[...] = res[...]
    if not last:
        halo_col.wait()
        halo_row.wait_sent()
        halo_col.wait_sent()
        pad_out[...] = pad[...]


def exchange(rows, cols, last, scans, obj, probe, near, grad, pgrad):
    tile, full = obj.shape[1], grad.shape[1]
    half = (full - tile) // 2
    channels = grad.shape[0]
    steps = plan(phases(rows, cols), pgrad.shape[0] // STREAMS)
    boxes = STREAMS * sum(n * ((1 << len(group)) - 1) for group, _, n in steps)
    most = max((1 << len(group)) - 1 for group, _, _ in steps)
    vmem = pl.BlockSpec(memory_space=pltpu.VMEM)
    out_shape = [jax.ShapeDtypeStruct(obj.shape, F32), jax.ShapeDtypeStruct(probe.shape, F32)]
    scratch = [
        pltpu.VMEM((2, channels, full, half), F32),
        pltpu.VMEM((channels, full, tile), F32),
        pltpu.VMEM((2, channels, half, tile), F32),
        pltpu.VMEM(obj.shape, F32),
        pltpu.VMEM(pgrad.shape, F32),
        pltpu.VMEM((boxes,) + pgrad.shape[1:], F32),
        pltpu.VMEM(probe.shape, F32),
        pltpu.SemaphoreType.DMA((2, 4)),
        pltpu.SemaphoreType.DMA((STREAMS, 2, len(steps), most)),
        pltpu.SemaphoreType.DMA((STREAMS, 2, len(steps), most)),
    ]
    if not last:
        out_shape.append(jax.ShapeDtypeStruct((2, full, full), F32))
        scratch += [pltpu.VMEM((2, full, full), F32), pltpu.SemaphoreType.DMA((2, 4))]
    return pl.pallas_call(
        lambda *refs: exchange_kernel(rows, cols, last, scans, *refs),
        out_shape=out_shape,
        in_specs=[vmem] * 5,
        out_specs=[vmem] * len(out_shape),
        scratch_shapes=scratch,
        compiler_params=pltpu.CompilerParams(
            collective_id=2 if last else 1,
            has_side_effects=True,
            vmem_limit_bytes=48 * 1024 * 1024,
        ),
    )(obj, probe, near, grad, pgrad)


def split_np(table):
    high = table.astype(np.float32).astype(ml_dtypes.bfloat16)
    low = (table - high.astype(np.float64)).astype(np.float32).astype(ml_dtypes.bfloat16)
    return [high, low]


def tables(side):
    half = side // 2
    n = np.arange(half)[:, None]
    k = np.arange(half)[None, :]
    pieces = []
    for odd in (0, 1):
        angle = 2.0 * math.pi * ((n * (2 * k + odd)) % side) / side
        cos, sin = np.cos(angle) / math.sqrt(side), np.sin(angle) / math.sqrt(side)
        forward = np.block([[cos, -sin], [sin, cos]])
        pieces += split_np(forward) + split_np(forward.T)
    return np.stack(pieces)


def order_table(side):
    half = side // 2
    place = np.concatenate([2 * np.arange(half), 2 * np.arange(half) + 1])
    table = np.zeros((side, side), np.float32)
    table[place, np.arange(side)] = 1.0
    return np.stack([table, table.T]).astype(ml_dtypes.bfloat16)


def split(x):
    high = x.astype(BF16)
    return high, (x - high.astype(F32)).astype(BF16)


def dot(a, b):
    return jnp.dot(a, b, preferred_element_type=F32)


def right(x, tab, at):
    high, low = split(x)
    return dot(high, tab[at]) + (dot(high, tab[at + 1]) + dot(low, tab[at]))


def left(tab, at, x):
    high, low = split(x)
    return dot(tab[at], high) + (dot(tab[at + 1], high) + dot(tab[at], low))


FE, GE, FO, GO = 0, 2, 4, 6


def forward(re, im, tab):
    h = re.shape[1] // 2
    even = right(jnp.concatenate([re[:, :h] + re[:, h:], im[:, :h] + im[:, h:]], 1), tab, FE)
    odd = right(jnp.concatenate([re[:, :h] - re[:, h:], im[:, :h] - im[:, h:]], 1), tab, FO)
    re = jnp.concatenate([even[:, :h], odd[:, :h]], 1)
    im = jnp.concatenate([even[:, h:], odd[:, h:]], 1)
    even = left(tab, GE, jnp.concatenate([re[:h] + re[h:], im[:h] + im[h:]], 0))
    odd = left(tab, GO, jnp.concatenate([re[:h] - re[h:], im[:h] - im[h:]], 0))
    return (
        jnp.concatenate([even[:h], odd[:h]], 0),
        jnp.concatenate([even[h:], odd[h:]], 0),
    )


def inverse(re, im, tab):
    h = re.shape[1] // 2
    even = left(tab, FE, jnp.concatenate([re[:h], im[:h]], 0))
    odd = left(tab, FO, jnp.concatenate([re[h:], im[h:]], 0))
    low, high = even + odd, even - odd
    re = jnp.concatenate([low[:h], high[:h]], 0)
    im = jnp.concatenate([low[h:], high[h:]], 0)
    even = right(jnp.concatenate([re[:, :h], im[:, :h]], 1), tab, GE)
    odd = right(jnp.concatenate([re[:, h:], im[:, h:]], 1), tab, GO)
    low, high = even + odd, even - odd
    return (
        jnp.concatenate([low[:, :h], high[:, :h]], 1),
        jnp.concatenate([low[:, h:], high[:, h:]], 1),
    )


def whole(tiles, at, side):
    blocks = tiles.shape[0] * tiles.shape[2] // side
    per = tiles.shape[0] // blocks
    return jnp.concatenate(
        [tiles[j * per:(j + 1) * per, at].reshape(side, -1) for j in range(blocks)], 1
    )


def put(tiles, at, value, add):
    width = tiles.shape[3]
    per = value.shape[0] // tiles.shape[2]
    for j in range(value.shape[1] // width):
        part = value[:, j * width:(j + 1) * width].reshape(per, tiles.shape[2], width)
        span = slice(j * per, (j + 1) * per)
        tiles[span, at] = tiles[span, at] + part if add else part


def step_kernel(starts, obj, tiles, amp, tab, order, grad, pgrad, wide):
    side = amp.shape[1]
    full = obj.shape[1]
    modes = tiles.shape[1] // 2
    scans = amp.shape[0]
    probe = {(c, k): whole(tiles, c * modes + k, side) for c in range(2) for k in range(modes)}
    wide[...] = jnp.zeros_like(wide)
    for s in range(scans):
        row, col = starts[s, 0] + side // 2, starts[s, 1] + side // 2
        back_row, back_col = lax.rem(full - row, full), lax.rem(full - col, full)
        win = []
        for ch in range(2):
            x = pltpu.roll(obj[ch], back_row, 0)[:side]
            win.append(pltpu.roll(x, back_col, 1)[:, :side])
        wr, wi = win
        ordered = jnp.zeros((side, side), F32)
        for part in split(amp[s]):
            ordered = ordered + dot(order[1], dot(part, order[0]).astype(BF16))
        fars = []
        intensity = jnp.zeros((side, side), F32)
        for k in range(modes):
            pr, pi = probe[0, k], probe[1, k]
            fr, fi = forward(pr * wr - pi * wi, pr * wi + pi * wr, tab)
            intensity = intensity + fr * fr + fi * fi
            fars.append((fr, fi))
        factor = ordered / jnp.maximum(jnp.sqrt(intensity), FLOOR) - 1.0
        gr = jnp.zeros((side, side), F32)
        gi = jnp.zeros((side, side), F32)
        for k in range(modes):
            br, bi = inverse(fars[k][0] * factor, fars[k][1] * factor, tab)
            pr, pi = probe[0, k], probe[1, k]
            gr = gr + pr * br + pi * bi
            gi = gi + pr * bi - pi * br
            for ch, value in enumerate((wr * br + wi * bi, wr * bi - wi * br)):
                at = ch * modes + k
                put(pgrad, at, value, s > 0)
        put(pgrad, 2 * modes, wr * wr + wi * wi, s > 0)
        for ch, value in enumerate((gr, gi)):
            wide[:side, :side] = value
            x = pltpu.roll(pltpu.roll(wide[...], col, 1), row, 0)
            grad[ch] = x if s == 0 else grad[ch] + x


def step(starts, padded, probe, measured, tab, order):
    side = measured.shape[1]
    full = padded.shape[1]
    vmem = pl.BlockSpec(memory_space=pltpu.VMEM)
    flops = 2 * side**3 * 12 * 8
    return pl.pallas_call(
        step_kernel,
        out_shape=(
            jax.ShapeDtypeStruct((2, full, full), F32),
            jax.ShapeDtypeStruct((probe.shape[0], probe.shape[1] + 1) + probe.shape[2:], F32),
        ),
        in_specs=[pl.BlockSpec(memory_space=pltpu.SMEM)] + [vmem] * 5,
        out_specs=(vmem, vmem),
        scratch_shapes=[pltpu.VMEM((full, full), F32)],
        compiler_params=pltpu.CompilerParams(vmem_limit_bytes=48 * 1024 * 1024),
        cost_estimate=pl.CostEstimate(flops=flops, bytes_accessed=6 << 20, transcendentals=0),
    )(starts, padded, probe, measured, tab, order)


def local(object_field, probe, amplitudes, offsets):
    side = probe.shape[2]
    half = side // 2
    rows, cols = lax.axis_size("row"), lax.axis_size("col")
    starts = offsets[0, 0]
    scans = starts.shape[0]
    measured = amplitudes[0, 0]
    tab = jnp.asarray(tables(side))
    order = jnp.asarray(order_table(side))
    channels = probe.shape[0] * probe.shape[1]
    cut = (channels, side // 8, 8, side // 128, 128)
    tiles = probe.reshape(cut).transpose(3, 1, 0, 2, 4).reshape(-1, channels, 8, 128)
    offs = jnp.broadcast_to(starts.reshape(-1, 1), (2 * scans, 128))
    padded, near = halo(rows, cols, object_field, offs, half)
    for iteration in range(ITERS):
        last = iteration + 1 == ITERS
        grad, pgrad = step(starts, padded, tiles, measured, tab, order)
        out = exchange(rows, cols, last, scans, object_field, tiles, near, grad, pgrad)
        object_field, tiles = out[:2]
        if not last:
            padded = out[2]
    back = tiles.reshape(side // 128, side // 8, channels, 8, 128).transpose(2, 1, 3, 0, 4)
    return object_field, back.reshape(probe.shape)


def solution(mesh):
    return jax.shard_map(
        local,
        mesh=mesh,
        in_specs=(
            P(None, "row", "col"),
            P(),
            P("row", "col", None, None, None),
            P("row", "col", None, None),
        ),
        out_specs=(P(None, "row", "col"), P()),
        check_vma=False,
    )
```
